512 devices in a mesh: rollout: 64 (over z, y_hi, core), tensor: 8 (over y_lo, x).
Axes of the slice: x: 4, y: 8 (y_hi: 4, y_lo: 2; y = y_hi * 2 + y_lo), z: 8, core: 2. Of those that a mesh axis runs over, the one named last changes fastest.
Arguments:
- tokens: bfloat16 [16384, 8192], P('rollout', 'tensor'), may hold values from -6 to 6
- base_key_value_weight: bfloat16 [8192, 2, 1024], P(None, None, 'tensor'), may hold values from -0.0625 to 0.0625
- key_value_bias: bfloat16 [2, 1024], P(None, 'tensor'), may hold values from -3 to 3
- adapter_down_blocks: bfloat16 [8192, 2, 128], P('rollout'), may hold values from -0.0625 to 0.0625
- adapter_up_blocks: bfloat16 [2, 128, 1024], P(None, 'rollout', 'tensor'), may hold values from -0.29882812 to 0.29882812
- owner_shard_lookup: int32 [64], replicated, may hold values from 0 to 63, each once
- lengths: int32 [64, 8], P('rollout'), may hold values from 1 to 128, 256 in all within a row
- routes: int32 [16384], P('rollout'), may hold values from 0 to 63, as said below
Outputs:
- kv_cache: bfloat16 [32768, 2, 1024], P('rollout', None, 'tensor')
The draws below stay inside these ranges and needn't reach their ends.
Inputs may be any that keep to these rules, and one draw needn't show every extreme that they name: `owner_shard_lookup`: a permutation of the rollout indices. `routes`: the rows of one group name each destination at most 8 times; one destination, drawn from the seed, is named exactly 8 times by every group.
All inputs are finite; a program needn't handle non-finite values.
Results may differ from the reference program's by a relative error of at most 0.0048.
Values may be sent and summed in bfloat16 or wider, within the bound.
No kernel may reach another device: no remote copies, remote signals or barrier semaphores. Data moves between devices by JAX's collectives and lax.ppermute only.
A program may use at most 128 MiB of HBM per device.

```python
import math
import jax
import jax.numpy as jnp
import numpy as np
from jax import lax

MODEL_FEATURES = 8192
HEAD = 128
UPDATE_RANK = 128
ROWS_SRC = 256
SEGS = 8
ROLLOUT_GROUPS = 64
KEY_VALUE_WIDTH = 1024
CAP = 8
SLOTS = 512
SEG_MOST = 128


def draw_routes(key, part):
    key = jax.random.fold_in(key, 11)
    hottest = jax.random.randint(jax.random.fold_in(key, 0), (), 0, ROLLOUT_GROUPS)

    def one_source(source):
        source_key = jax.random.fold_in(key, source + 1)
        pieces = []
        for index in range(CAP):
            pieces.append(jax.random.permutation(jax.random.fold_in(source_key, index), ROLLOUT_GROUPS - 1))
        offsets = jnp.concatenate(pieces)[:ROWS_SRC - CAP]
        others = (hottest + 1 + offsets) % ROLLOUT_GROUPS
        listed = jnp.concatenate([jnp.full((CAP,), hottest, jnp.int32), others.astype(jnp.int32)])
        shuffle = jax.random.permutation(jax.random.fold_in(source_key, CAP + 7), ROWS_SRC)
        return listed[shuffle]
    return jax.vmap(one_source)(jnp.arange(ROLLOUT_GROUPS)).reshape(-1).astype(jnp.int32)


def level_of(stream_key, shape, cuts, least, largest):
    level = 1.0
    for axis_at, blocks in cuts:
        steps = jax.random.uniform(jax.random.fold_in(jax.random.fold_in(stream_key, 6), axis_at), (blocks,), jnp.float32, least / len(cuts), largest / len(cuts))
        level = level * jnp.repeat(jnp.exp(steps), shape[axis_at] // blocks).reshape((-1,) + (1,) * (len(shape) - 1 - axis_at))
    return level


def split_up(amount, total, reach, skew):
    loads = [(1 << 20) // math.isqrt(standing ** skew) + 1 for standing in range(2, amount + 1)]
    surplus, given = total - reach - (amount - 1), [1] * (amount - 1)
    while surplus > 0:
        free = [i for i in range(amount - 1) if given[i] < reach]
        pool, budget = sum([loads[i] for i in free]), surplus
        for i in free:
            more = min(reach - given[i], max(1, budget * loads[i] // pool), surplus)
            given[i] = given[i] + more
            surplus = surplus - more
    return np.array([reach] + given)


def ragged_sizes(own_key, count, total, reach, slope):
    if count == 2:
        one = jax.random.randint(own_key, (), max(1, total - reach), min(reach, total - 1) + 1)
        return jnp.stack([one, total - one])
    sizes = jnp.asarray(split_up(count, total, reach, slope), jnp.int32)
    couples = (count - 1) // 2
    donor, taker = sizes[1:1 + 2 * couples:2], sizes[2:2 + 2 * couples:2]
    margin = jnp.minimum(donor - 1, reach - taker)
    shifted = jax.random.randint(jax.random.fold_in(own_key, 1), (couples,), 0, 1 << 20) % (margin + 1)
    sizes = sizes.at[1:1 + 2 * couples:2].set(donor - shifted).at[2:2 + 2 * couples:2].set(taker + shifted)
    return sizes[jax.random.permutation(jax.random.fold_in(own_key, 2), count)]


def normal_values(own_key, shape, deviation, limit, cuts=(), kind=jnp.bfloat16):
    array = jax.random.normal(own_key, shape, jnp.float32) * deviation
    if len(cuts) > 0:
        array = level_of(own_key, shape, cuts, -0.22, 0.18) * array
    return jnp.clip(array, min=-limit, max=limit).astype(kind)


def setup_inputs(seed: int = 0) -> dict:
    key_list = jax.random.split(jax.random.key(seed), 9)
    tokens = normal_values(key_list[0], (ROLLOUT_GROUPS * ROWS_SRC, MODEL_FEATURES), 1.0, 6.0, ((0, 64), (1, 8)))
    base_key_value_weight = normal_values(key_list[1], (MODEL_FEATURES, 2, KEY_VALUE_WIDTH), MODEL_FEATURES ** -0.5, 0.0625, ((2, 8),))
    key_value_bias = normal_values(key_list[2], (2, KEY_VALUE_WIDTH), 0.5, 3.0, ((1, 8),))
    adapter_down_blocks = normal_values(key_list[3], (MODEL_FEATURES, 2, UPDATE_RANK), MODEL_FEATURES ** -0.5, 0.0625, ((0, 64),))
    adapter_up_blocks = normal_values(key_list[4], (2, UPDATE_RANK, KEY_VALUE_WIDTH), 0.05, 0.29882812, ((1, 64), (2, 8)))
    owner_shard_lookup = jax.random.permutation(key_list[5], ROLLOUT_GROUPS).astype(jnp.int32)
    lengths = jax.vmap(lambda own: ragged_sizes(own, SEGS, ROWS_SRC, SEG_MOST, 2))(jax.random.split(key_list[6], ROLLOUT_GROUPS)).reshape((ROLLOUT_GROUPS, SEGS)).astype(jnp.int32)
    routes = draw_routes(jax.random.fold_in(key_list[8], 71), 0)
    return dict(tokens=tokens, base_key_value_weight=base_key_value_weight, key_value_bias=key_value_bias, adapter_down_blocks=adapter_down_blocks, adapter_up_blocks=adapter_up_blocks, owner_shard_lookup=owner_shard_lookup, lengths=lengths, routes=routes)


adapter_scale = 2.0
rope_base = 1000000.0


def positions_of(lengths_row, row_count):
    ends = jnp.cumsum(lengths_row)
    starts = ends - lengths_row
    index = jnp.arange(row_count, dtype=jnp.int32)
    begins = jnp.max(jnp.where(starts[None, :] <= index[:, None], starts[None, :], 0), axis=1)
    return (index - begins).astype(jnp.int32)


def rotate(keys, places):
    half_width = HEAD // 2
    frequency = rope_base ** (-(jnp.arange(half_width, dtype=jnp.float32) * 2.0) / HEAD)
    angles = places.astype(jnp.float32)[:, None] * frequency[None, :]
    cosine = jnp.cos(angles)[:, None, :]
    sine = jnp.sin(angles)[:, None, :]
    shaped = keys.reshape(keys.shape[0], -1, HEAD)
    first = shaped[..., :half_width]
    second = shaped[..., half_width:]
    turned = jnp.concatenate([first * cosine - second * sine, second * cosine + first * sine], axis=-1)
    return turned.reshape(keys.shape)


def finish_rows(summed, places, key_value_bias):
    width = key_value_bias.shape[1]
    shaped = summed.reshape(summed.shape[0], 2, width) + key_value_bias.astype(jnp.float32)[None]
    keys = rotate(shaped[:, 0], places)
    return jnp.stack([keys, shaped[:, 1]], axis=1)


def reference(tokens, base_key_value_weight, key_value_bias, adapter_down_blocks, adapter_up_blocks, owner_shard_lookup, lengths, routes):
    inverse_permutation = jnp.zeros((ROLLOUT_GROUPS,), jnp.int32).at[owner_shard_lookup].set(jnp.arange(ROLLOUT_GROUPS, dtype=jnp.int32))
    down_factor = adapter_down_blocks.reshape(ROLLOUT_GROUPS, MODEL_FEATURES // ROLLOUT_GROUPS, 2, UPDATE_RANK)[inverse_permutation].reshape(MODEL_FEATURES, 2, UPDATE_RANK)
    up_factor = adapter_up_blocks.reshape(2, ROLLOUT_GROUPS, UPDATE_RANK // ROLLOUT_GROUPS, KEY_VALUE_WIDTH)[:, inverse_permutation].reshape(2, UPDATE_RANK, KEY_VALUE_WIDTH)
    weight_update = jnp.einsum("ohd,hde->ohe", down_factor.astype(jnp.float32), up_factor.astype(jnp.float32))
    merged_weight = (base_key_value_weight.astype(jnp.float32) + adapter_scale * weight_update).astype(jnp.bfloat16)
    merged_flat = merged_weight.reshape(MODEL_FEATURES, 2 * KEY_VALUE_WIDTH)
    places = jax.vmap(lambda row: positions_of(row, ROWS_SRC))(lengths)
    token_blocks = tokens.reshape(ROLLOUT_GROUPS, ROWS_SRC, MODEL_FEATURES)

    def project_group(inputs):
        block, block_places = inputs
        summed = jnp.dot(block, merged_flat, preferred_element_type=jnp.float32)
        return finish_rows(summed, block_places, key_value_bias).astype(jnp.bfloat16)

    cache_rows = lax.map(project_group, (token_blocks, places))
    target = routes.reshape(ROLLOUT_GROUPS, ROWS_SRC)
    matches = (target[:, :, None] == jnp.arange(ROLLOUT_GROUPS, dtype=jnp.int32)[None, None, :]).astype(jnp.int32)
    order_in = jnp.sum((jnp.cumsum(matches, axis=1) - matches) * matches, axis=2)
    sources = jnp.arange(ROLLOUT_GROUPS, dtype=jnp.int32)[:, None]
    slot = (target * SLOTS + sources * CAP + order_in).astype(jnp.int32)
    result = jnp.zeros((ROLLOUT_GROUPS * SLOTS, 2, KEY_VALUE_WIDTH), jnp.bfloat16)
    return result.at[slot.reshape(-1)].set(cache_rows.reshape(ROLLOUT_GROUPS * ROWS_SRC, 2, KEY_VALUE_WIDTH))
```

```python
import jax
import jax.numpy as jnp
from jax import lax
from jax.experimental import pallas as pl
from jax.experimental.pallas import tpu as pltpu
from jax.sharding import PartitionSpec as P

HEAD = 128
GROUPS = 64
RANK = 128
MODEL = 8192
ROWS = 256
CAP = 8
X = 4
Y_HI = 4
Z = 8

adapter_scale = 2.0
rope_base = 1000000.0

HALF = MODEL // 2
QUARTER = MODEL // 4
WIDE = 2 * HEAD
SLICE = 2 * RANK // X
PART = SLICE // 2
SENT = PART + 8

X_GROUPS = [[0, 1, 2, 3], [4, 5, 6, 7]]
SIBLING = [(a, a ^ 1) for a in range(GROUPS)]
Y_PARTNER = [(a, (a + X) % (2 * X)) for a in range(2 * X)]


def flat_index(z, y, core, x):
    return ((z * Y_HI + y // 2) * 2 + core) * (2 * X) + (y % 2) * X + x


WEIGHT_HOP = [
    (
        flat_index(z, y, core, x),
        flat_index(z, (y + (1 if core == 0 else -1)) % (2 * Y_HI), core, x),
    )
    for z in range(Z)
    for y in range(2 * Y_HI)
    for core in range(2)
    for x in range(X)
]

VMEM_LIMIT = 40 * 1024 * 1024


def vmem(count):
    return [pl.BlockSpec(memory_space=pltpu.VMEM)] * count


def smem(count):
    return [pl.BlockSpec(memory_space=pltpu.SMEM)] * count


def factors_kernel(lookup_ref, own_ref, near_ref, far_ref, down_ref, up_ref, inverse, up_rows):
    y, core = own_ref[0], own_ref[1]

    @pl.loop(0, GROUPS)
    def _(owner):
        inverse[lookup_ref[owner]] = owner

    for local in range(GROUPS // 2):
        owner = inverse[(GROUPS // 2) * y + local]
        mine = near_ref[owner, 0:PART, :]
        other = far_ref[owner, 0:PART, :]
        columns = slice(local * 128, (local + 1) * 128)
        down_ref[0:PART, columns] = jnp.where(core == 0, mine, other)
        down_ref[PART:SLICE, columns] = jnp.where(core == 0, other, mine)
    for shard in range(GROUPS):
        rows = near_ref[inverse[shard], PART:SENT, :].astype(jnp.float32)
        up_rows[2 * shard : 2 * shard + 2, :] = rows[0:2]
        up_rows[RANK + 2 * shard : RANK + 2 * shard + 2, :] = rows[2:4]
    up_ref[...] = up_rows[...].astype(jnp.bfloat16)


def factors(lookup, own, near, far):
    return pl.pallas_call(
        factors_kernel,
        out_shape=(
            jax.ShapeDtypeStruct((SLICE, HALF), jnp.bfloat16),
            jax.ShapeDtypeStruct((2 * RANK, HEAD), jnp.bfloat16),
        ),
        in_specs=smem(2) + vmem(2),
        out_specs=tuple(vmem(2)),
        scratch_shapes=[
            pltpu.SMEM((GROUPS,), jnp.int32),
            pltpu.VMEM((2 * RANK, HEAD), jnp.float32),
        ],
        compiler_params=pltpu.CompilerParams(vmem_limit_bytes=VMEM_LIMIT),
        name="factors",
    )(lookup, own, near, far)


def low_rank_kernel(tokens_ref, down_ref, out_ref):
    total = None
    for step in range(X):
        part = lax.dot_general(
            down_ref[:, step * 1024 : (step + 1) * 1024],
            tokens_ref[step],
            (((1,), (1,)), ((), ())),
            preferred_element_type=jnp.float32,
        )
        total = part if total is None else total + part
    out_ref[...] = total.astype(jnp.bfloat16)


def low_rank(tokens, down):
    return pl.pallas_call(
        low_rank_kernel,
        out_shape=jax.ShapeDtypeStruct((SLICE, ROWS), jnp.bfloat16),
        in_specs=vmem(2),
        out_specs=vmem(1)[0],
        compiler_params=pltpu.CompilerParams(vmem_limit_bytes=VMEM_LIMIT),
        name="low_rank",
    )(tokens, down)


def project_kernel(tokens_ref, weight_ref, out_ref):
    total = None
    for step in range(X):
        part = jnp.dot(
            tokens_ref[step],
            weight_ref[step * 1024 : (step + 1) * 1024, :],
            preferred_element_type=jnp.float32,
        )
        total = part if total is None else total + part
    out_ref[...] = total.astype(out_ref.dtype)


def project(tokens, weight, dtype):
    return pl.pallas_call(
        project_kernel,
        out_shape=jax.ShapeDtypeStruct((ROWS, WIDE), dtype),
        in_specs=vmem(2),
        out_specs=vmem(1)[0],
        compiler_params=pltpu.CompilerParams(vmem_limit_bytes=VMEM_LIMIT),
        name="project",
    )(tokens, weight)


def finish_kernel(own_ref, met_ref, low_ref, up_ref, bias_ref, cos_ref, sin_ref, slot_ref, out_ref):
    base = own_ref[...] + met_ref[...].astype(jnp.float32)
    made = []
    for side in range(2):
        update = None
        for y in range(2):
            for part in range(2):
                first = side * RANK + part * SLICE
                term = lax.dot_general(
                    low_ref[y * X + 2 * side + part],
                    up_ref[first : first + SLICE, :],
                    (((0,), (0,)), ((), ())),
                    preferred_element_type=jnp.float32,
                )
                update = term if update is None else update + term
        made.append(
            base[:, side * HEAD : (side + 1) * HEAD]
            + adapter_scale * update
            + bias_ref[side : side + 1, :].astype(jnp.float32)
        )
    keys = made[0]
    keys = keys * cos_ref[...] + pltpu.roll(keys, HEAD // 2, 1) * sin_ref[...]
    rows = jnp.concatenate([keys, made[1]], axis=1).astype(jnp.bfloat16)
    slots = lax.broadcasted_iota(jnp.int32, (GROUPS * CAP, ROWS), 0)
    chosen = jnp.where(slots == slot_ref[...], 1.0, 0.0).astype(jnp.bfloat16)
    placed = jnp.dot(chosen, rows, preferred_element_type=jnp.float32).astype(jnp.bfloat16)
    out_ref[...] = placed.reshape(GROUPS, CAP, WIDE)


def finish(own, met, low, up, bias, cosine, sine, slots):
    return pl.pallas_call(
        finish_kernel,
        out_shape=jax.ShapeDtypeStruct((GROUPS, CAP, WIDE), jnp.bfloat16),
        in_specs=vmem(8),
        out_specs=vmem(1)[0],
        compiler_params=pltpu.CompilerParams(vmem_limit_bytes=VMEM_LIMIT),
        name="finish",
    )(own, met, low, up, bias, cosine, sine, slots)


def positions_of(lengths_row):
    ends = jnp.cumsum(lengths_row)
    starts = ends - lengths_row
    index = jnp.arange(ROWS, dtype=jnp.int32)
    begins = jnp.max(jnp.where(starts[None, :] <= index[:, None], starts[None, :], 0), axis=1)
    return index - begins


def turn_tables(places):
    half_width = HEAD // 2
    frequency = rope_base ** (-(jnp.arange(half_width, dtype=jnp.float32) * 2.0) / HEAD)
    angles = places.astype(jnp.float32)[:, None] * frequency[None, :]
    cosine, sine = jnp.cos(angles), jnp.sin(angles)
    return jnp.concatenate([cosine, cosine], 1), jnp.concatenate([-sine, sine], 1)


def slot_index(target):
    index = jnp.arange(ROWS, dtype=jnp.int32)
    earlier = (target[:, None] == target[None, :]) & (index[:, None] < index[None, :])
    return target * CAP + jnp.sum(earlier.astype(jnp.int32), axis=0)


def body(tokens, weight, bias, down_blocks, up_blocks, lookup, lengths, routes):
    lane = lax.axis_index("tensor")
    y, x = lane // X, lane % X
    core = lax.axis_index("rollout") % 2

    down_turned = down_blocks.transpose(1, 2, 0).reshape(X, 2, PART, 128)
    down_sent = lax.dynamic_index_in_dim(down_turned, x, 0, keepdims=False)
    up_sent = jnp.broadcast_to(up_blocks.reshape(1, 4, HEAD), (2, 4, HEAD))
    sent = jnp.concatenate([down_sent, up_sent, jnp.zeros((2, 4, HEAD), jnp.bfloat16)], 1)
    sent = jnp.broadcast_to(sent[None], (GROUPS // 2, 2, SENT, HEAD)).reshape(GROUPS, SENT, HEAD)
    near = lax.all_to_all(sent, "rollout", 0, 0, tiled=True)

    gathered = lax.all_gather(tokens, "tensor", axis=0, axis_index_groups=X_GROUPS)

    weight_sent = lax.dynamic_slice_in_dim(weight, (1 - y) * HALF + core * QUARTER, QUARTER, 0)
    weight_near = lax.ppermute(
        weight_sent.reshape(QUARTER, WIDE), ("rollout", "tensor"), WEIGHT_HOP
    )
    weight_far = lax.ppermute(weight_near, "rollout", SIBLING)
    weight_met = jnp.where(
        core == 0,
        jnp.concatenate([weight_near, weight_far], 0),
        jnp.concatenate([weight_far, weight_near], 0),
    )
    weight_own = lax.dynamic_slice_in_dim(weight, y * HALF, HALF, 0).reshape(HALF, WIDE)

    far = lax.ppermute(near, "rollout", SIBLING)
    own = jnp.stack([y, core]).astype(jnp.int32)
    down, up = factors(lookup, own, near, far)

    cosine, sine = turn_tables(positions_of(lengths[0]))
    slots = slot_index(routes).reshape(1, ROWS)

    partial_met = project(gathered, weight_met, jnp.bfloat16)
    partial_in = lax.ppermute(partial_met, "tensor", Y_PARTNER)
    low = low_rank(gathered, down)
    low_all = lax.all_to_all(
        jnp.broadcast_to(low[None], (2 * X, SLICE, ROWS)), "tensor", 0, 0, tiled=True
    )
    partial_own = project(gathered, weight_own, jnp.float32)
    outgoing = finish(partial_own, partial_in, low_all, up, bias, cosine, sine, slots)
    arrived = lax.all_to_all(outgoing, "rollout", 0, 0, tiled=True)
    return arrived.reshape(GROUPS * CAP, 2, HEAD)


def solution(mesh):
    in_specs = (
        P("rollout", "tensor"),
        P(None, None, "tensor"),
        P(None, "tensor"),
        P("rollout", None, None),
        P(None, "rollout", "tensor"),
        P(),
        P("rollout", None),
        P("rollout"),
    )
    out_specs = P("rollout", None, "tensor")
    return jax.shard_map(body, mesh=mesh, in_specs=in_specs, out_specs=out_specs, check_vma=False)
```

```python
import jax
import jax.numpy as jnp
from jax import lax
from jax.experimental import pallas as pl
from jax.experimental.pallas import tpu as pltpu
from jax.sharding import PartitionSpec as P

HEAD = 128
GROUPS = 64
RANK = 128
MODEL = 8192
ROWS = 256
CAP = 8
X = 4
Y_HI = 4
Z = 8

adapter_scale = 2.0
rope_base = 1000000.0

HALF = MODEL // 2
QUARTER = MODEL // 4
WIDE = 2 * HEAD
SLICE = 2 * RANK // X
SENT = SLICE + 8
BLOCK = MODEL // (2 * X)

SAME_CORE = [list(range(core, GROUPS, 2)) for core in range(2)]
SIBLING = [(a, a ^ 1) for a in range(GROUPS)]
X_HOP = [[(a, a // X * X + (a - hop) % X) for a in range(2 * X)] for hop in range(X)]
Y_PARTNER = [(a, (a + X) % (2 * X)) for a in range(2 * X)]


def flat_index(z, y, core, x):
    return ((z * Y_HI + y // 2) * 2 + core) * (2 * X) + (y % 2) * X + x


WEIGHT_HOP = [
    (
        flat_index(z, y, core, x),
        flat_index(z, (y + (1 if core == 0 else -1)) % (2 * Y_HI), core, x),
    )
    for z in range(Z)
    for y in range(2 * Y_HI)
    for core in range(2)
    for x in range(X)
]

VMEM_LIMIT = 16 * 1024 * 1024


def vmem(count):
    return [pl.BlockSpec(memory_space=pltpu.VMEM)] * count


def smem(count):
    return [pl.BlockSpec(memory_space=pltpu.SMEM)] * count


def factors_kernel(lookup_ref, own_ref, near_ref, far_ref, down_ref, up_ref, inverse, up_rows):
    y, core = own_ref[0], own_ref[2]

    @pl.loop(0, GROUPS)
    def _(owner):
        inverse[lookup_ref[owner]] = owner

    for local in range(GROUPS // 2):
        owner = inverse[(GROUPS // 2) * y + local]
        rows = jnp.where(
            owner % 2 == core, near_ref[owner // 2, 0:SLICE, :], far_ref[owner // 2, 0:SLICE, :]
        )
        down_ref[:, local * 128 : (local + 1) * 128] = rows
    for shard in range(GROUPS):
        owner = inverse[shard]
        rows = jnp.where(
            owner % 2 == core, near_ref[owner // 2, SLICE:SENT, :], far_ref[owner // 2, SLICE:SENT, :]
        ).astype(jnp.float32)
        up_rows[2 * shard : 2 * shard + 2, :] = rows[0:2]
        up_rows[RANK + 2 * shard : RANK + 2 * shard + 2, :] = rows[2:4]
    up_ref[...] = up_rows[...].astype(jnp.bfloat16)


def factors(lookup, own, near, far):
    return pl.pallas_call(
        factors_kernel,
        out_shape=(
            jax.ShapeDtypeStruct((SLICE, HALF), jnp.bfloat16),
            jax.ShapeDtypeStruct((2 * RANK, HEAD), jnp.bfloat16),
        ),
        in_specs=smem(2) + vmem(2),
        out_specs=tuple(vmem(2)),
        scratch_shapes=[
            pltpu.SMEM((GROUPS,), jnp.int32),
            pltpu.VMEM((2 * RANK, HEAD), jnp.float32),
        ],
        compiler_params=pltpu.CompilerParams(vmem_limit_bytes=VMEM_LIMIT),
        name="factors",
    )(lookup, own, near, far)


def block_start(own_ref, hop):
    return pl.multiple_of(((own_ref[1] + hop) % X) * BLOCK, BLOCK)


def low_rank_kernel(own_ref, *refs):
    down_ref, out_ref = refs[X:]
    total = None
    for hop in range(X):
        part = lax.dot_general(
            down_ref[:, pl.ds(block_start(own_ref, hop), BLOCK)],
            refs[hop][...],
            (((1,), (1,)), ((), ())),
            preferred_element_type=jnp.float32,
        )
        total = part if total is None else total + part
    out_ref[...] = total.astype(jnp.bfloat16)


def low_rank(own, blocks, down):
    return pl.pallas_call(
        low_rank_kernel,
        out_shape=jax.ShapeDtypeStruct((SLICE, ROWS), jnp.bfloat16),
        in_specs=smem(1) + vmem(X + 1),
        out_specs=vmem(1)[0],
        compiler_params=pltpu.CompilerParams(vmem_limit_bytes=VMEM_LIMIT),
        name="low_rank",
    )(own, *blocks, down)


def project_met_kernel(own_ref, *refs):
    near_ref, far_ref, out_ref, total = refs[X:]
    core = own_ref[2]
    total[...] = jnp.zeros_like(total)
    for hop in range(X):
        source = (own_ref[1] + hop) % X
        rows = pl.ds(pl.multiple_of((source % 2) * BLOCK, BLOCK), BLOCK)

        @pl.when(source // 2 == core)
        def _():
            total[...] += jnp.dot(
                refs[hop][...], near_ref[rows, :], preferred_element_type=jnp.float32
            )

        @pl.when(source // 2 != core)
        def _():
            total[...] += jnp.dot(
                refs[hop][...], far_ref[rows, :], preferred_element_type=jnp.float32
            )

    out_ref[...] = total[...].astype(jnp.bfloat16)


def project_met(own, blocks, near, far):
    return pl.pallas_call(
        project_met_kernel,
        out_shape=jax.ShapeDtypeStruct((ROWS, WIDE), jnp.bfloat16),
        in_specs=smem(1) + vmem(X + 2),
        out_specs=vmem(1)[0],
        scratch_shapes=[pltpu.VMEM((ROWS, WIDE), jnp.float32)],
        compiler_params=pltpu.CompilerParams(vmem_limit_bytes=VMEM_LIMIT),
        name="project_met",
    )(own, *blocks, near, far)


def project_own_kernel(own_ref, *refs):
    weight_ref, out_ref = refs[X:]
    total = None
    for hop in range(X):
        part = jnp.dot(
            refs[hop][...],
            weight_ref[pl.ds(block_start(own_ref, hop), BLOCK), :],
            preferred_element_type=jnp.float32,
        )
        total = part if total is None else total + part
    out_ref[...] = total


def project_own(own, blocks, weight):
    return pl.pallas_call(
        project_own_kernel,
        out_shape=jax.ShapeDtypeStruct((ROWS, WIDE), jnp.float32),
        in_specs=smem(1) + vmem(X + 1),
        out_specs=vmem(1)[0],
        compiler_params=pltpu.CompilerParams(vmem_limit_bytes=VMEM_LIMIT),
        name="project_own",
    )(own, *blocks, weight)


def finish_kernel(own_ref, met_ref, low_ref, up_ref, bias_ref, cos_ref, sin_ref, slot_ref, out_ref):
    base = own_ref[...] + met_ref[...].astype(jnp.float32)
    made = []
    for side in range(2):
        update = None
        for y in range(2):
            for part in range(2):
                first = side * RANK + part * SLICE
                term = lax.dot_general(
                    low_ref[y * X + 2 * side + part],
                    up_ref[first : first + SLICE, :],
                    (((0,), (0,)), ((), ())),
                    preferred_element_type=jnp.float32,
                )
                update = term if update is None else update + term
        made.append(
            base[:, side * HEAD : (side + 1) * HEAD]
            + adapter_scale * update
            + bias_ref[side : side + 1, :].astype(jnp.float32)
        )
    keys = made[0]
    keys = keys * cos_ref[...] + pltpu.roll(keys, HEAD // 2, 1) * sin_ref[...]
    rows = jnp.concatenate([keys, made[1]], axis=1).astype(jnp.bfloat16)
    slots = lax.broadcasted_iota(jnp.int32, (GROUPS * CAP, ROWS), 0)
    chosen = jnp.where(slots == slot_ref[...], 1.0, 0.0).astype(jnp.bfloat16)
    placed = jnp.dot(chosen, rows, preferred_element_type=jnp.float32).astype(jnp.bfloat16)
    out_ref[...] = placed.reshape(GROUPS, CAP, WIDE)


def finish(own, met, low, up, bias, cosine, sine, slots):
    return pl.pallas_call(
        finish_kernel,
        out_shape=jax.ShapeDtypeStruct((GROUPS, CAP, WIDE), jnp.bfloat16),
        in_specs=vmem(8),
        out_specs=vmem(1)[0],
        compiler_params=pltpu.CompilerParams(vmem_limit_bytes=VMEM_LIMIT),
        name="finish",
    )(own, met, low, up, bias, cosine, sine, slots)


def positions_of(lengths_row):
    ends = jnp.cumsum(lengths_row)
    starts = ends - lengths_row
    index = jnp.arange(ROWS, dtype=jnp.int32)
    begins = jnp.max(jnp.where(starts[None, :] <= index[:, None], starts[None, :], 0), axis=1)
    return index - begins


def turn_tables(places):
    half_width = HEAD // 2
    frequency = rope_base ** (-(jnp.arange(half_width, dtype=jnp.float32) * 2.0) / HEAD)
    angles = places.astype(jnp.float32)[:, None] * frequency[None, :]
    cosine, sine = jnp.cos(angles), jnp.sin(angles)
    return jnp.concatenate([cosine, cosine], 1), jnp.concatenate([-sine, sine], 1)


def slot_index(target):
    index = jnp.arange(ROWS, dtype=jnp.int32)
    earlier = (target[:, None] == target[None, :]) & (index[:, None] < index[None, :])
    return target * CAP + jnp.sum(earlier.astype(jnp.int32), axis=0)


def body(tokens, weight, bias, down_blocks, up_blocks, lookup, lengths, routes):
    lane = lax.axis_index("tensor")
    y, x = lane // X, lane % X
    core = lax.axis_index("rollout") % 2
    own = jnp.stack([y, x, core]).astype(jnp.int32)

    weight_sent = lax.dynamic_slice_in_dim(weight, (1 - y) * HALF + core * QUARTER, QUARTER, 0)
    weight_sent = weight_sent.reshape(QUARTER, WIDE)
    weight_near = lax.ppermute(weight_sent, ("rollout", "tensor"), WEIGHT_HOP)
    blocks = [tokens] + [lax.ppermute(tokens, "tensor", X_HOP[hop]) for hop in range(1, X)]
    weight_far = lax.ppermute(weight_near, "rollout", SIBLING)

    down_blocks, up_blocks, _ = lax.optimization_barrier((down_blocks, up_blocks, weight_sent))
    down_turned = down_blocks.transpose(1, 2, 0).reshape(X, SLICE, 128)
    down_sent = lax.dynamic_index_in_dim(down_turned, x, 0, keepdims=False)
    sent = jnp.concatenate(
        [down_sent, up_blocks.reshape(4, HEAD), jnp.zeros((4, HEAD), jnp.bfloat16)], 0
    )
    sent = jnp.broadcast_to(sent[None], (GROUPS // 2, SENT, HEAD))
    near = lax.all_to_all(sent, "rollout", 0, 0, tiled=True, axis_index_groups=SAME_CORE)

    partial_met = project_met(own, blocks, weight_near, weight_far)
    partial_in = lax.ppermute(partial_met, "tensor", Y_PARTNER)
    weight_own = lax.dynamic_slice_in_dim(weight, y * HALF, HALF, 0).reshape(HALF, WIDE)
    partial_own = project_own(own, blocks, weight_own)
    cosine, sine = turn_tables(positions_of(lengths[0]))
    slots = slot_index(routes).reshape(1, ROWS)

    near, cosine, sine, slots, partial_own, partial_in = lax.optimization_barrier(
        (near, cosine, sine, slots, partial_own, partial_in)
    )
    far = lax.ppermute(near, "rollout", SIBLING)
    down, up = factors(lookup, own, near, far)

    low = low_rank(own, blocks, down)
    low_all = lax.all_to_all(
        jnp.broadcast_to(low[None], (2 * X, SLICE, ROWS)), "tensor", 0, 0, tiled=True
    )
    outgoing = finish(partial_own, partial_in, low_all, up, bias, cosine, sine, slots)
    arrived = lax.all_to_all(outgoing, "rollout", 0, 0, tiled=True)
    return arrived.reshape(GROUPS * CAP, 2, HEAD)


def solution(mesh):
    in_specs = (
        P("rollout", "tensor"),
        P(None, None, "tensor"),
        P(None, "tensor"),
        P("rollout", None, None),
        P(None, "rollout", "tensor"),
        P(),
        P("rollout", None),
        P("rollout"),
    )
    out_specs = P("rollout", None, "tensor")
    return jax.shard_map(body, mesh=mesh, in_specs=in_specs, out_specs=out_specs, check_vma=False)
```

```python
import functools

import jax
import jax.numpy as jnp
import numpy as np
from jax import lax
from jax.experimental import pallas as pl
from jax.experimental.pallas import tpu as pltpu
from jax.sharding import PartitionSpec as P

HEAD = 128
GROUPS = 64
RANK = 128
MODEL = 8192
ROWS = 256
CAP = 8
X = 4

adapter_scale = 2.0
rope_base = 1000000.0

SHARE = 2 * X
WIDE = 2 * HEAD
SLICE = 2 * RANK // SHARE
SENT = SLICE + 8
BLOCK = MODEL // SHARE

SAME_CORE = [list(range(core, GROUPS, 2)) for core in range(2)]
SIBLING = [(a, a ^ 1) for a in range(GROUPS)]
X_HOP = [[(a, a // X * X + (a - hop) % X) for a in range(2 * X)] for hop in range(X)]
Y_PARTNER = [(a, (a + X) % (2 * X)) for a in range(2 * X)]


VMEM_LIMIT = 16 * 1024 * 1024
BUFFERS = 4

BESIDE = pl.CostEstimate(flops=8 * 10**9, bytes_accessed=0, transcendentals=0)


def vmem(count):
    return [pl.BlockSpec(memory_space=pltpu.VMEM)] * count


def in_hbm(array):
    return pltpu.with_memory_space_constraint(array, pltpu.HBM)


def hbm(count):
    return [pl.BlockSpec(memory_space=pltpu.HBM)] * count


def smem(count):
    return [pl.BlockSpec(memory_space=pltpu.SMEM)] * count


def share_kernel(
    own_ref,
    lengths_ref,
    rate_ref,
    down_hbm,
    up_hbm,
    out_ref,
    turn_ref,
    down_ref,
    up_ref,
    wide,
    turned,
    done,
):
    down_copy = pltpu.make_async_copy(down_hbm, down_ref, done.at[0])
    up_copy = pltpu.make_async_copy(up_hbm, up_ref, done.at[1])
    down_copy.start()
    up_copy.start()
    row = lax.broadcasted_iota(jnp.int32, (ROWS, HEAD), 0)
    begins = jnp.zeros((ROWS, HEAD), jnp.int32)
    start = jnp.int32(0)
    for piece in range(lengths_ref.shape[1]):
        begins = jnp.where(row >= start, jnp.maximum(begins, start), begins)
        start = start + lengths_ref[0, piece]
    angles = (row - begins).astype(jnp.float32) * rate_ref[...]
    low_half = lax.broadcasted_iota(jnp.int32, (ROWS, HEAD), 1) < HEAD // 2
    turn_ref[...] = jnp.cos(jnp.where(low_half, angles, angles - np.float32(np.pi / 2)))
    down_copy.wait()
    up_copy.wait()
    lane = own_ref[0] * X + own_ref[1]
    wide[...] = down_ref[...].astype(jnp.float32)
    turned[...] = wide[pl.ds(lane // X, 128, stride=2), :].T
    first = pl.multiple_of((lane % X) * SLICE, SLICE)
    down = turned[pl.ds(first, SLICE), :].astype(jnp.bfloat16)
    up = jnp.concatenate([up_ref[...], jnp.zeros((SENT - SLICE - 4, HEAD), jnp.bfloat16)], 0)
    sent = jnp.concatenate([down, up], 0)
    for target in range(GROUPS // 2):
        out_ref[target] = sent


def share(own, lengths, down_rows, up_rows):
    half_rate = rope_base ** (-(np.arange(HEAD // 2, dtype=np.float32) * 2.0) / HEAD)
    rate = jnp.asarray(np.concatenate([half_rate, half_rate])[None], jnp.float32)
    return pl.pallas_call(
        share_kernel,
        out_shape=(
            jax.ShapeDtypeStruct((GROUPS // 2, SENT, HEAD), jnp.bfloat16),
            pltpu.HBM((ROWS, HEAD), jnp.float32),
        ),
        in_specs=smem(2) + vmem(1) + hbm(2),
        out_specs=tuple(vmem(2)),
        scratch_shapes=[
            pltpu.VMEM((2 * 128, RANK), jnp.bfloat16),
            pltpu.VMEM((4, HEAD), jnp.bfloat16),
            pltpu.VMEM((2 * 128, RANK), jnp.float32),
            pltpu.VMEM((RANK, 128), jnp.float32),
            pltpu.SemaphoreType.DMA((2,)),
        ],
        compiler_params=pltpu.CompilerParams(vmem_limit_bytes=VMEM_LIMIT),
        name="share",
    )(own, in_hbm(lengths), in_hbm(rate), in_hbm(down_rows), in_hbm(up_rows))


def source_of(own_ref, place):
    return (own_ref[0] + place // X) % 2 * X + (own_ref[1] + place) % X


def low_part(own_ref, blocks, down_ref, places):
    total = None
    for block, place in zip(blocks, places):
        first = pl.multiple_of(source_of(own_ref, place) * BLOCK, BLOCK)
        part = lax.dot_general(
            block[...],
            down_ref[:, pl.ds(first, BLOCK)],
            (((1,), (1,)), ((), ())),
            preferred_element_type=jnp.float32,
        )
        total = part if total is None else total + part
    return total


def low_begin_kernel(places, lookup_ref, own_ref, near_ref, far_ref, tokens_ref, *refs):
    down_ref, begun_ref, up_ref, inverse, up_rows, held, done = refs[len(places) - 1 :]
    copy = pltpu.make_async_copy(tokens_ref, held, done)
    copy.start()
    core = own_ref[2]
    for owner in range(GROUPS):
        inverse[lookup_ref[owner]] = owner
    for shard in range(GROUPS):
        owner = inverse[shard]
        rows = jnp.where(owner % 2 == core, near_ref[owner // 2], far_ref[owner // 2])
        down_ref[:, shard * 128 : (shard + 1) * 128] = rows[0:SLICE]
        rows = rows[SLICE:SENT].astype(jnp.float32)
        up_rows[2 * shard : 2 * shard + 2, :] = rows[0:2]
        up_rows[RANK + 2 * shard : RANK + 2 * shard + 2, :] = rows[2:4]
    up_ref[...] = up_rows[...].astype(jnp.bfloat16)
    copy.wait()
    begun_ref[...] = low_part(own_ref, [*refs[: len(places) - 1], held], down_ref, places)


def low_begin(lookup, own, near, far, blocks, places):
    return pl.pallas_call(
        functools.partial(low_begin_kernel, places),
        out_shape=(
            jax.ShapeDtypeStruct((SLICE, MODEL), jnp.bfloat16),
            jax.ShapeDtypeStruct((ROWS, SLICE), jnp.float32),
            pltpu.HBM((2 * RANK, HEAD), jnp.bfloat16),
        ),
        in_specs=smem(2) + vmem(2) + hbm(1) + vmem(len(places) - 1),
        out_specs=tuple(vmem(3)),
        scratch_shapes=[
            pltpu.SMEM((GROUPS,), jnp.int32),
            pltpu.VMEM((2 * RANK, HEAD), jnp.float32),
            pltpu.VMEM((ROWS, BLOCK), jnp.bfloat16),
            pltpu.SemaphoreType.DMA,
        ],
        compiler_params=pltpu.CompilerParams(vmem_limit_bytes=VMEM_LIMIT),
        name="low_begin",
    )(
        in_hbm(lookup),
        own,
        near,
        far,
        in_hbm(blocks[0]),
        *[blocks[place] for place in places if place],
    )


def low_end_kernel(places, own_ref, down_ref, begun_ref, *refs):
    total = begun_ref[...] + low_part(own_ref, refs[:-1], down_ref, places)
    low = total.T.astype(jnp.bfloat16)
    for target in range(SHARE):
        refs[-1][target] = low


def low_end(own, down, begun, blocks, places):
    return pl.pallas_call(
        functools.partial(low_end_kernel, places),
        out_shape=pltpu.HBM((SHARE, SLICE, ROWS), jnp.bfloat16),
        in_specs=smem(1) + vmem(2 + len(places)),
        out_specs=vmem(1)[0],
        compiler_params=pltpu.CompilerParams(vmem_limit_bytes=VMEM_LIMIT),
        name="low_end",
    )(own, down, begun, *[blocks[place] for place in places])


def weight_copies(own_ref, weight_ref, weights, done, places):
    copies = []
    for at, place in enumerate(places):
        first = pl.multiple_of(source_of(own_ref, place) * (2 * BLOCK), 2 * BLOCK)
        copies.append(
            pltpu.make_async_copy(
                weight_ref.at[pl.ds(first, 2 * BLOCK)],
                weights.at[at % BUFFERS],
                done.at[at % BUFFERS],
            )
        )
    return copies


def project_blocks(copies, blocks, weights):
    total = None
    for at, (copy, block) in enumerate(zip(copies, blocks)):
        copy.wait()
        part = jnp.dot(
            block[...],
            weights[at % BUFFERS].reshape(BLOCK, WIDE),
            preferred_element_type=jnp.float32,
        )
        total = part if total is None else total + part
        if at + BUFFERS < len(copies):
            copies[at + BUFFERS].start()
    return total


def begin_kernel(places, own_ref, weight_ref, *refs):
    out_ref, weights, done = refs[len(places) :]
    copies = weight_copies(own_ref, weight_ref, weights, done, places)
    for copy in copies[:BUFFERS]:
        copy.start()
    out_ref[...] = project_blocks(copies, refs[: len(places)], weights)


def begin(own, blocks, places, weight_rows):
    return pl.pallas_call(
        functools.partial(begin_kernel, places),
        out_shape=pltpu.HBM((ROWS, WIDE), jnp.float32),
        in_specs=smem(1) + hbm(1) + vmem(len(places)),
        out_specs=vmem(1)[0],
        scratch_shapes=[
            pltpu.VMEM((BUFFERS, 2 * BLOCK, HEAD), jnp.bfloat16),
            pltpu.SemaphoreType.DMA((BUFFERS,)),
        ],
        cost_estimate=BESIDE,
        compiler_params=pltpu.CompilerParams(vmem_limit_bytes=VMEM_LIMIT),
        name="begin",
    )(own, weight_rows, *[blocks[place] for place in places])


def project_kernel(
    places, own_ref, weight_ref, tokens_ref, turn_ref, up_ref, begun_ref, bias_ref, *refs
):
    out_ref, weights, tokens, turn, up, begun, weight_done, done = refs[len(places) - 1 :]
    copies = weight_copies(own_ref, weight_ref, weights, weight_done, places)
    for copy in copies[:BUFFERS]:
        copy.start()
    small = [
        pltpu.make_async_copy(from_ref, to_ref, done.at[at])
        for at, (from_ref, to_ref) in enumerate(
            [(turn_ref, turn), (up_ref, up), (begun_ref, begun), (tokens_ref, tokens)]
        )
    ]
    for copy in small:
        copy.start()
    for copy in small:
        copy.wait()
    table = turn[...]
    swapped = pltpu.roll(table, HEAD // 2, 1)
    low_half = lax.broadcasted_iota(jnp.int32, (ROWS, HEAD), 1) < HEAD // 2
    cosine = jnp.where(low_half, table, swapped)
    sine = jnp.where(low_half, -swapped, table)
    out_ref[:, WIDE : WIDE + HEAD] = cosine
    out_ref[:, WIDE + HEAD : 2 * WIDE] = sine
    out_ref[:, 2 * WIDE :] = up[...].astype(jnp.float32)
    total = begun[...] + project_blocks(copies, [*refs[: len(places) - 1], tokens], weights)
    keys = total[:, :HEAD] + bias_ref[0:1, :].astype(jnp.float32)
    out_ref[:, :HEAD] = keys * cosine + pltpu.roll(keys, HEAD // 2, 1) * sine
    out_ref[:, HEAD:WIDE] = total[:, HEAD:] + bias_ref[1:2, :].astype(jnp.float32)


def project(own, blocks, places, weight_rows, turn, up, begun, bias):
    return pl.pallas_call(
        functools.partial(project_kernel, places),
        out_shape=jax.ShapeDtypeStruct((ROWS, 2 * WIDE + HEAD), jnp.float32),
        in_specs=smem(1) + hbm(5) + vmem(len(places)),
        out_specs=vmem(1)[0],
        scratch_shapes=[
            pltpu.VMEM((BUFFERS, 2 * BLOCK, HEAD), jnp.bfloat16),
            pltpu.VMEM((ROWS, BLOCK), jnp.bfloat16),
            pltpu.VMEM((ROWS, HEAD), jnp.float32),
            pltpu.VMEM((2 * RANK, HEAD), jnp.bfloat16),
            pltpu.VMEM((ROWS, WIDE), jnp.float32),
            pltpu.SemaphoreType.DMA((BUFFERS,)),
            pltpu.SemaphoreType.DMA((4,)),
        ],
        compiler_params=pltpu.CompilerParams(vmem_limit_bytes=VMEM_LIMIT),
        name="project",
    )(
        own,
        weight_rows,
        in_hbm(blocks[0]),
        in_hbm(turn),
        in_hbm(up),
        in_hbm(begun),
        in_hbm(bias),
        *[blocks[place] for place in places if place],
    )


def finish_kernel(made_ref, low_ref, slot_ref, out_ref, placed):
    updates = []
    for side in range(2):
        ranks = slice(side * RANK, (side + 1) * RANK)
        updates.append(
            adapter_scale
            * lax.dot_general(
                low_ref[ranks, :],
                made_ref[ranks, 2 * WIDE :].astype(jnp.bfloat16),
                (((0,), (0,)), ((), ())),
                preferred_element_type=jnp.float32,
            )
        )
    keys = updates[0]
    cosine, sine = made_ref[:, WIDE : WIDE + HEAD], made_ref[:, WIDE + HEAD : 2 * WIDE]
    keys = keys * cosine + pltpu.roll(keys, HEAD // 2, 1) * sine
    rows = made_ref[:, :WIDE] + jnp.concatenate([keys, updates[1]], axis=1)
    rows = rows.astype(jnp.bfloat16)
    slots = lax.broadcasted_iota(jnp.int32, (GROUPS * CAP, ROWS), 0)
    chosen = jnp.where(slots == slot_ref[...], 1.0, 0.0).astype(jnp.bfloat16)
    slot_rows = jnp.dot(chosen, rows, preferred_element_type=jnp.float32)
    for side in range(2):
        placed[pl.ds(side, GROUPS * CAP, stride=2), :] = slot_rows[
            :, side * HEAD : (side + 1) * HEAD
        ]
    out_ref[...] = placed[...].astype(jnp.bfloat16)


def finish(made, low, slots):
    return pl.pallas_call(
        finish_kernel,
        out_shape=jax.ShapeDtypeStruct((2 * GROUPS * CAP, HEAD), jnp.bfloat16),
        in_specs=vmem(3),
        out_specs=vmem(1)[0],
        scratch_shapes=[pltpu.VMEM((2 * GROUPS * CAP, HEAD), jnp.float32)],
        compiler_params=pltpu.CompilerParams(vmem_limit_bytes=VMEM_LIMIT),
        name="finish",
    )(made, low, slots)


def slots_kernel(routes_ref, slot_ref):
    target = routes_ref[...]
    later = jnp.broadcast_to(target.astype(jnp.float32), (ROWS, ROWS))
    below = lax.broadcasted_iota(jnp.int32, (ROWS, ROWS), 0)
    after = lax.broadcasted_iota(jnp.int32, (ROWS, ROWS), 1)
    same = jnp.where((later.T == later) & (below < after), 1, 0)
    slot_ref[...] = target * CAP + jnp.sum(same, axis=0, keepdims=True)


def slots_of(routes):
    return pl.pallas_call(
        slots_kernel,
        out_shape=jax.ShapeDtypeStruct((1, ROWS), jnp.int32),
        in_specs=vmem(1),
        out_specs=vmem(1)[0],
        cost_estimate=BESIDE,
        compiler_params=pltpu.CompilerParams(vmem_limit_bytes=VMEM_LIMIT),
        name="slots",
    )(in_hbm(routes.reshape(1, ROWS)))


def body(tokens, weight, bias, down_blocks, up_blocks, lookup, lengths, routes):
    lane = lax.axis_index("tensor")
    y, x = lane // X, lane % X
    core = lax.axis_index("rollout") % 2
    own = jnp.stack([y, x, core]).astype(jnp.int32)

    weight_rows = in_hbm(weight.reshape(2 * MODEL, HEAD))

    def along_x(block, hop):
        return lax.ppermute(block, "tensor", X_HOP[hop])

    def across_y(block):
        return lax.ppermute(block, "tensor", Y_PARTNER)

    met = across_y(tokens)
    far_x, next_x, last_x = along_x(tokens, 2), along_x(tokens, 1), along_x(tokens, 3)

    sent, turn = share(
        own, lengths, down_blocks.reshape(2 * 128, RANK), up_blocks.reshape(4, HEAD)
    )
    near = lax.all_to_all(sent, "rollout", 0, 0, tiled=True, axis_index_groups=SAME_CORE)
    far = lax.ppermute(near, "rollout", SIBLING)

    met, far_x = lax.optimization_barrier((met, far_x))
    met_far = across_y(far_x)
    met_next, met_last = along_x(met, 1), along_x(met, 3)
    blocks = [tokens, next_x, far_x, last_x, met, met_next, met_far, met_last]
    early, late = (1, 2, 3, 4, 0), (6, 5, 7)
    down, begun, up = low_begin(lookup, own, near, far, blocks, early)
    slots = slots_of(routes)
    started = begin(own, blocks, (1, 2), weight_rows)
    met_far, met_next, met_last, down, begun, up, slots, started = lax.optimization_barrier(
        (met_far, met_next, met_last, down, begun, up, slots, started)
    )
    blocks[5:] = [met_next, met_far, met_last]
    low = low_end(own, down, begun, blocks, late)
    low_all = lax.all_to_all(low, "tensor", 0, 0, tiled=True).reshape(2 * RANK, ROWS)
    made = project(own, blocks, (3, 4, 5, 6, 7, 0), weight_rows, turn, up, started, bias)
    outgoing = finish(made, low_all, slots)
    arrived = lax.all_to_all(outgoing, "rollout", 0, 0, tiled=True)
    return arrived.reshape(GROUPS * CAP, 2, HEAD)


def solution(mesh):
    in_specs = (
        P("rollout", "tensor"),
        P(None, None, "tensor"),
        P(None, "tensor"),
        P("rollout", None, None),
        P(None, "rollout", "tensor"),
        P(),
        P("rollout", None),
        P("rollout"),
    )
    out_specs = P("rollout", None, "tensor")
    return jax.shard_map(body, mesh=mesh, in_specs=in_specs, out_specs=out_specs, check_vma=False)
```

```python
import functools

import jax
import jax.numpy as jnp
import numpy as np
from jax import lax
from jax.experimental import pallas as pl
from jax.experimental.pallas import tpu as pltpu
from jax.sharding import PartitionSpec as P

HEAD = 128
GROUPS = 64
RANK = 128
MODEL = 8192
ROWS = 256
CAP = 8
X = 4

adapter_scale = 2.0
rope_base = 1000000.0

SHARE = 2 * X
WIDE = 2 * HEAD
SLICE = 2 * RANK // SHARE
SENT = SLICE + 8
BLOCK = MODEL // SHARE

SAME_CORE = [list(range(core, GROUPS, 2)) for core in range(2)]
SIBLING = [(a, a ^ 1) for a in range(GROUPS)]
X_HOP = [[(a, a // X * X + (a - hop) % X) for a in range(2 * X)] for hop in range(X)]
Y_PARTNER = [(a, (a + X) % (2 * X)) for a in range(2 * X)]


VMEM_LIMIT = 16 * 1024 * 1024
BUFFERS = 4
FIRST = (1, 2, 0)
REST = (3, 4, 6, 5, 7)

BESIDE = pl.CostEstimate(flops=8 * 10**9, bytes_accessed=0, transcendentals=0)


def vmem(count):
    return [pl.BlockSpec(memory_space=pltpu.VMEM)] * count


def in_hbm(array):
    return pltpu.with_memory_space_constraint(array, pltpu.HBM)


def hbm(count):
    return [pl.BlockSpec(memory_space=pltpu.HBM)] * count


def smem(count):
    return [pl.BlockSpec(memory_space=pltpu.SMEM)] * count


def share_kernel(
    own_ref,
    lengths_ref,
    rate_ref,
    down_hbm,
    up_hbm,
    out_ref,
    turn_ref,
    down_ref,
    up_ref,
    wide,
    turned,
    done,
):
    down_copy = pltpu.make_async_copy(down_hbm, down_ref, done.at[0])
    up_copy = pltpu.make_async_copy(up_hbm, up_ref, done.at[1])
    down_copy.start()
    up_copy.start()
    row = lax.broadcasted_iota(jnp.int32, (ROWS, HEAD), 0)
    begins = jnp.zeros((ROWS, HEAD), jnp.int32)
    start = jnp.int32(0)
    for piece in range(lengths_ref.shape[1]):
        begins = jnp.where(row >= start, jnp.maximum(begins, start), begins)
        start = start + lengths_ref[0, piece]
    angles = (row - begins).astype(jnp.float32) * rate_ref[...]
    low_half = lax.broadcasted_iota(jnp.int32, (ROWS, HEAD), 1) < HEAD // 2
    turn_ref[...] = jnp.cos(jnp.where(low_half, angles, angles - np.float32(np.pi / 2)))
    down_copy.wait()
    up_copy.wait()
    lane = own_ref[0] * X + own_ref[1]
    wide[...] = down_ref[...].astype(jnp.float32)
    turned[...] = wide[pl.ds(lane // X, 128, stride=2), :].T
    first = pl.multiple_of((lane % X) * SLICE, SLICE)
    down = turned[pl.ds(first, SLICE), :].astype(jnp.bfloat16)
    up = jnp.concatenate([up_ref[...], jnp.zeros((SENT - SLICE - 4, HEAD), jnp.bfloat16)], 0)
    sent = jnp.concatenate([down, up], 0)
    for target in range(GROUPS // 2):
        out_ref[target] = sent


def share(own, lengths, down_rows, up_rows):
    half_rate = rope_base ** (-(np.arange(HEAD // 2, dtype=np.float32) * 2.0) / HEAD)
    rate = jnp.asarray(np.concatenate([half_rate, half_rate])[None], jnp.float32)
    return pl.pallas_call(
        share_kernel,
        out_shape=(
            jax.ShapeDtypeStruct((GROUPS // 2, SENT, HEAD), jnp.bfloat16),
            pltpu.HBM((ROWS, HEAD), jnp.float32),
        ),
        in_specs=smem(2) + vmem(1) + hbm(2),
        out_specs=tuple(vmem(2)),
        scratch_shapes=[
            pltpu.VMEM((2 * 128, RANK), jnp.bfloat16),
            pltpu.VMEM((4, HEAD), jnp.bfloat16),
            pltpu.VMEM((2 * 128, RANK), jnp.float32),
            pltpu.VMEM((RANK, 128), jnp.float32),
            pltpu.SemaphoreType.DMA((2,)),
        ],
        compiler_params=pltpu.CompilerParams(vmem_limit_bytes=VMEM_LIMIT),
        name="share",
    )(own, in_hbm(lengths), in_hbm(rate), in_hbm(down_rows), in_hbm(up_rows))


def source_of(own_ref, place):
    return (own_ref[0] + place // X) % 2 * X + (own_ref[1] + place) % X


def inverse_kernel(lookup_ref, inverse_ref):
    for owner in range(GROUPS):
        inverse_ref[lookup_ref[owner]] = owner


def inverse_of(lookup):
    return pl.pallas_call(
        inverse_kernel,
        out_shape=pltpu.HBM((GROUPS,), jnp.int32),
        in_specs=smem(1),
        out_specs=smem(1)[0],
        cost_estimate=BESIDE,
        compiler_params=pltpu.CompilerParams(vmem_limit_bytes=VMEM_LIMIT),
        name="inverse",
    )(in_hbm(lookup))


def low_part(own_ref, blocks, down_ref, places):
    total = None
    for block, place in zip(blocks, places):
        first = pl.multiple_of(source_of(own_ref, place) * BLOCK, BLOCK)
        part = lax.dot_general(
            block[...],
            down_ref[:, pl.ds(first, BLOCK)],
            (((1,), (1,)), ((), ())),
            preferred_element_type=jnp.float32,
        )
        total = part if total is None else total + part
    return total


def weight_copies(own_ref, weight_ref, weights, done, places):
    copies = []
    for at, place in enumerate(places):
        first = pl.multiple_of(source_of(own_ref, place) * (2 * BLOCK), 2 * BLOCK)
        copies.append(
            pltpu.make_async_copy(
                weight_ref.at[pl.ds(first, 2 * BLOCK)],
                weights.at[at % BUFFERS],
                done.at[at % BUFFERS],
            )
        )
    return copies


def project_blocks(copies, blocks, weights):
    total = None
    for at, (copy, block) in enumerate(zip(copies, blocks)):
        copy.wait()
        part = jnp.dot(
            block[...],
            weights[at % BUFFERS].reshape(BLOCK, WIDE),
            preferred_element_type=jnp.float32,
        )
        total = part if total is None else total + part
        if at + BUFFERS < len(copies):
            copies[at + BUFFERS].start()
    return total


def low_begin_kernel(
    places, inverse_ref, own_ref, near_ref, far_ref, weight_ref, tokens_ref, *refs
):
    down_ref, begun_ref, up_ref, base_ref, up_rows, held, weights, done, weight_done = refs[
        len(places) - 1 :
    ]
    copies = weight_copies(own_ref, weight_ref, weights, weight_done, FIRST)
    for weight_copy in copies[:BUFFERS]:
        weight_copy.start()
    copy = pltpu.make_async_copy(tokens_ref, held, done)
    copy.start()
    core = own_ref[2]
    for shard in range(GROUPS):
        owner = inverse_ref[shard]
        rows = jnp.where(owner % 2 == core, near_ref[owner // 2], far_ref[owner // 2])
        down_ref[:, shard * 128 : (shard + 1) * 128] = rows[0:SLICE]
        rows = rows[SLICE:SENT].astype(jnp.float32)
        up_rows[2 * shard : 2 * shard + 2, :] = rows[0:2]
        up_rows[RANK + 2 * shard : RANK + 2 * shard + 2, :] = rows[2:4]
    up_ref[...] = up_rows[...].astype(jnp.bfloat16)
    copy.wait()
    blocks = [*refs[: len(places) - 1], held]
    begun_ref[...] = low_part(own_ref, blocks, down_ref, places)
    firsts = [blocks[places.index(place)] for place in FIRST]
    base_ref[...] = project_blocks(copies, firsts, weights)


def low_begin(inverse, own, near, far, weight_rows, blocks, places):
    return pl.pallas_call(
        functools.partial(low_begin_kernel, places),
        out_shape=(
            jax.ShapeDtypeStruct((SLICE, MODEL), jnp.bfloat16),
            jax.ShapeDtypeStruct((ROWS, SLICE), jnp.float32),
            pltpu.HBM((2 * RANK, HEAD), jnp.bfloat16),
            pltpu.HBM((ROWS, WIDE), jnp.float32),
        ),
        in_specs=smem(2) + vmem(2) + hbm(2) + vmem(len(places) - 1),
        out_specs=tuple(vmem(4)),
        scratch_shapes=[
            pltpu.VMEM((2 * RANK, HEAD), jnp.float32),
            pltpu.VMEM((ROWS, BLOCK), jnp.bfloat16),
            pltpu.VMEM((BUFFERS, 2 * BLOCK, HEAD), jnp.bfloat16),
            pltpu.SemaphoreType.DMA,
            pltpu.SemaphoreType.DMA((BUFFERS,)),
        ],
        compiler_params=pltpu.CompilerParams(vmem_limit_bytes=VMEM_LIMIT),
        name="low_begin",
    )(
        in_hbm(inverse),
        own,
        near,
        far,
        weight_rows,
        in_hbm(blocks[0]),
        *[blocks[place] for place in places if place],
    )


def low_end_kernel(places, own_ref, down_ref, begun_ref, *refs):
    total = begun_ref[...] + low_part(own_ref, refs[:-1], down_ref, places)
    low = total.T.astype(jnp.bfloat16)
    for target in range(SHARE):
        refs[-1][target] = low


def low_end(own, down, begun, blocks, places):
    return pl.pallas_call(
        functools.partial(low_end_kernel, places),
        out_shape=pltpu.HBM((SHARE, SLICE, ROWS), jnp.bfloat16),
        in_specs=smem(1) + vmem(2 + len(places)),
        out_specs=vmem(1)[0],
        compiler_params=pltpu.CompilerParams(vmem_limit_bytes=VMEM_LIMIT),
        name="low_end",
    )(own, down, begun, *[blocks[place] for place in places])


def project_kernel(places, own_ref, weight_ref, turn_ref, up_ref, begun_ref, bias_ref, *refs):
    out_ref, weights, turn, up, begun, weight_done, done = refs[len(places) :]
    copies = weight_copies(own_ref, weight_ref, weights, weight_done, places)
    for copy in copies[:BUFFERS]:
        copy.start()
    small = [
        pltpu.make_async_copy(from_ref, to_ref, done.at[at])
        for at, (from_ref, to_ref) in enumerate(
            [(turn_ref, turn), (up_ref, up), (begun_ref, begun)]
        )
    ]
    for copy in small:
        copy.start()
    for copy in small:
        copy.wait()
    table = turn[...]
    swapped = pltpu.roll(table, HEAD // 2, 1)
    low_half = lax.broadcasted_iota(jnp.int32, (ROWS, HEAD), 1) < HEAD // 2
    cosine = jnp.where(low_half, table, swapped)
    sine = jnp.where(low_half, -swapped, table)
    out_ref[:, WIDE : WIDE + HEAD] = cosine
    out_ref[:, WIDE + HEAD : 2 * WIDE] = sine
    out_ref[:, 2 * WIDE :] = up[...].astype(jnp.float32)
    total = begun[...] + project_blocks(copies, refs[: len(places)], weights)
    keys = total[:, :HEAD] + bias_ref[0:1, :].astype(jnp.float32)
    out_ref[:, :HEAD] = keys * cosine + pltpu.roll(keys, HEAD // 2, 1) * sine
    out_ref[:, HEAD:WIDE] = total[:, HEAD:] + bias_ref[1:2, :].astype(jnp.float32)


def project(own, blocks, places, weight_rows, turn, up, begun, bias):
    return pl.pallas_call(
        functools.partial(project_kernel, places),
        out_shape=jax.ShapeDtypeStruct((ROWS, 2 * WIDE + HEAD), jnp.float32),
        in_specs=smem(1) + hbm(4) + vmem(len(places) + 1),
        out_specs=vmem(1)[0],
        scratch_shapes=[
            pltpu.VMEM((BUFFERS, 2 * BLOCK, HEAD), jnp.bfloat16),
            pltpu.VMEM((ROWS, HEAD), jnp.float32),
            pltpu.VMEM((2 * RANK, HEAD), jnp.bfloat16),
            pltpu.VMEM((ROWS, WIDE), jnp.float32),
            pltpu.SemaphoreType.DMA((BUFFERS,)),
            pltpu.SemaphoreType.DMA((3,)),
        ],
        compiler_params=pltpu.CompilerParams(vmem_limit_bytes=VMEM_LIMIT),
        name="project",
    )(
        own,
        weight_rows,
        in_hbm(turn),
        in_hbm(up),
        in_hbm(begun),
        in_hbm(bias),
        *[blocks[place] for place in places],
    )


def finish_kernel(made_ref, low_ref, slot_ref, out_ref, placed):
    updates = []
    for side in range(2):
        ranks = slice(side * RANK, (side + 1) * RANK)
        updates.append(
            adapter_scale
            * lax.dot_general(
                low_ref[ranks, :],
                made_ref[ranks, 2 * WIDE :].astype(jnp.bfloat16),
                (((0,), (0,)), ((), ())),
                preferred_element_type=jnp.float32,
            )
        )
    keys = updates[0]
    cosine, sine = made_ref[:, WIDE : WIDE + HEAD], made_ref[:, WIDE + HEAD : 2 * WIDE]
    keys = keys * cosine + pltpu.roll(keys, HEAD // 2, 1) * sine
    rows = made_ref[:, :WIDE] + jnp.concatenate([keys, updates[1]], axis=1)
    rows = rows.astype(jnp.bfloat16)
    slots = lax.broadcasted_iota(jnp.int32, (GROUPS * CAP, ROWS), 0)
    chosen = jnp.where(slots == slot_ref[...], 1.0, 0.0).astype(jnp.bfloat16)
    slot_rows = jnp.dot(chosen, rows, preferred_element_type=jnp.float32)
    for side in range(2):
        placed[pl.ds(side, GROUPS * CAP, stride=2), :] = slot_rows[
            :, side * HEAD : (side + 1) * HEAD
        ]
    out_ref[...] = placed[...].astype(jnp.bfloat16)


def finish(made, low, slots):
    return pl.pallas_call(
        finish_kernel,
        out_shape=jax.ShapeDtypeStruct((2 * GROUPS * CAP, HEAD), jnp.bfloat16),
        in_specs=vmem(3),
        out_specs=vmem(1)[0],
        scratch_shapes=[pltpu.VMEM((2 * GROUPS * CAP, HEAD), jnp.float32)],
        compiler_params=pltpu.CompilerParams(vmem_limit_bytes=VMEM_LIMIT),
        name="finish",
    )(made, low, slots)


def slots_kernel(routes_ref, slot_ref):
    target = routes_ref[...]
    later = jnp.broadcast_to(target.astype(jnp.float32), (ROWS, ROWS))
    below = lax.broadcasted_iota(jnp.int32, (ROWS, ROWS), 0)
    after = lax.broadcasted_iota(jnp.int32, (ROWS, ROWS), 1)
    same = jnp.where((later.T == later) & (below < after), 1, 0)
    slot_ref[...] = target * CAP + jnp.sum(same, axis=0, keepdims=True)


def slots_of(routes):
    return pl.pallas_call(
        slots_kernel,
        out_shape=jax.ShapeDtypeStruct((1, ROWS), jnp.int32),
        in_specs=vmem(1),
        out_specs=vmem(1)[0],
        cost_estimate=BESIDE,
        compiler_params=pltpu.CompilerParams(vmem_limit_bytes=VMEM_LIMIT),
        name="slots",
    )(in_hbm(routes.reshape(1, ROWS)))


def body(tokens, weight, bias, down_blocks, up_blocks, lookup, lengths, routes):
    lane = lax.axis_index("tensor")
    y, x = lane // X, lane % X
    core = lax.axis_index("rollout") % 2
    own = jnp.stack([y, x, core]).astype(jnp.int32)

    weight_rows = in_hbm(weight.reshape(2 * MODEL, HEAD))

    def along_x(block, hop):
        return lax.ppermute(block, "tensor", X_HOP[hop])

    def across_y(block):
        return lax.ppermute(block, "tensor", Y_PARTNER)

    met = across_y(tokens)
    far_x, next_x, last_x = along_x(tokens, 2), along_x(tokens, 1), along_x(tokens, 3)

    sent, turn = share(
        own, lengths, down_blocks.reshape(2 * 128, RANK), up_blocks.reshape(4, HEAD)
    )
    near = lax.all_to_all(sent, "rollout", 0, 0, tiled=True, axis_index_groups=SAME_CORE)
    far = lax.ppermute(near, "rollout", SIBLING)

    slots = slots_of(routes)
    far_x, slots = lax.optimization_barrier((far_x, slots))
    met_far = across_y(far_x)
    met_next, met_last = along_x(met, 1), along_x(met, 3)
    blocks = [tokens, next_x, far_x, last_x, met, met_next, met_far, met_last]
    early, late = (1, 2, 3, 4, 0), (6, 5, 7)
    down, begun, up, started = low_begin(
        inverse_of(lookup), own, near, far, weight_rows, blocks, early
    )
    met_far, met_next, met_last, down, begun, up, started, slots = lax.optimization_barrier(
        (met_far, met_next, met_last, down, begun, up, started, slots)
    )
    blocks[5:] = [met_next, met_far, met_last]
    low = low_end(own, down, begun, blocks, late)
    low_all = lax.all_to_all(low, "tensor", 0, 0, tiled=True).reshape(2 * RANK, ROWS)
    made = project(own, blocks, REST, weight_rows, turn, up, started, bias)
    outgoing = finish(made, low_all, slots)
    arrived = lax.all_to_all(outgoing, "rollout", 0, 0, tiled=True)
    return arrived.reshape(GROUPS * CAP, 2, HEAD)


def solution(mesh):
    in_specs = (
        P("rollout", "tensor"),
        P(None, None, "tensor"),
        P(None, "tensor"),
        P("rollout", None, None),
        P(None, "rollout", "tensor"),
        P(),
        P("rollout", None),
        P("rollout"),
    )
    out_specs = P("rollout", None, "tensor")
    return jax.shard_map(body, mesh=mesh, in_specs=in_specs, out_specs=out_specs, check_vma=False)
```

```python
import functools

import jax
import jax.numpy as jnp
import numpy as np
from jax import lax
from jax.experimental import pallas as pl
from jax.experimental.pallas import tpu as pltpu
from jax.sharding import PartitionSpec as P

HEAD = 128
GROUPS = 64
RANK = 128
MODEL = 8192
ROWS = 256
CAP = 8
X = 4

adapter_scale = 2.0
rope_base = 1000000.0

SHARE = 2 * X
WIDE = 2 * HEAD
SLICE = 2 * RANK // SHARE
SENT = SLICE + 8
BLOCK = MODEL // SHARE

SAME_CORE = [list(range(core, GROUPS, 2)) for core in range(2)]
SIBLING = [(a, a ^ 1) for a in range(GROUPS)]
X_HOP = [[(a, a // X * X + (a - hop) % X) for a in range(2 * X)] for hop in range(X)]
Y_PARTNER = [(a, (a + X) % (2 * X)) for a in range(2 * X)]


VMEM_LIMIT = 16 * 1024 * 1024
BUFFERS = 4
FIRST = (1, 2, 0)
REST = (3, 4, 6, 5, 7)

BESIDE = pl.CostEstimate(flops=8 * 10**9, bytes_accessed=0, transcendentals=0)


def vmem(count):
    return [pl.BlockSpec(memory_space=pltpu.VMEM)] * count


def in_hbm(array):
    return pltpu.with_memory_space_constraint(array, pltpu.HBM)


def hbm(count):
    return [pl.BlockSpec(memory_space=pltpu.HBM)] * count


def smem(count):
    return [pl.BlockSpec(memory_space=pltpu.SMEM)] * count


def share_kernel(own_ref, down_ref, up_ref, out_ref, wide, turned):
    lane = own_ref[0] * X + own_ref[1]
    wide[...] = down_ref[...].astype(jnp.float32)
    turned[...] = wide[pl.ds(lane // X, 128, stride=2), :].T
    first = pl.multiple_of((lane % X) * SLICE, SLICE)
    down = turned[pl.ds(first, SLICE), :].astype(jnp.bfloat16)
    up = jnp.concatenate([up_ref[...], jnp.zeros((SENT - SLICE - 4, HEAD), jnp.bfloat16)], 0)
    sent = jnp.concatenate([down, up], 0)
    for target in range(GROUPS // 2):
        out_ref[target] = sent


def share(own, down_rows, up_rows):
    return pl.pallas_call(
        share_kernel,
        out_shape=pltpu.HBM((GROUPS // 2, SENT, HEAD), jnp.bfloat16),
        in_specs=smem(1) + vmem(2),
        out_specs=vmem(1)[0],
        scratch_shapes=[
            pltpu.VMEM((2 * 128, RANK), jnp.float32),
            pltpu.VMEM((RANK, 128), jnp.float32),
        ],
        compiler_params=pltpu.CompilerParams(vmem_limit_bytes=VMEM_LIMIT),
        name="share",
    )(own, in_hbm(down_rows), in_hbm(up_rows))


def source_of(own_ref, place):
    return (own_ref[0] + place // X) % 2 * X + (own_ref[1] + place) % X


def inverse_kernel(lookup_ref, inverse_ref):
    for owner in range(GROUPS):
        inverse_ref[lookup_ref[owner]] = owner


def inverse_of(lookup):
    return pl.pallas_call(
        inverse_kernel,
        out_shape=pltpu.HBM((GROUPS,), jnp.int32),
        in_specs=smem(1),
        out_specs=smem(1)[0],
        cost_estimate=BESIDE,
        compiler_params=pltpu.CompilerParams(vmem_limit_bytes=VMEM_LIMIT),
        name="inverse",
    )(in_hbm(lookup))


def low_part(own_ref, blocks, down_ref, places):
    total = None
    for block, place in zip(blocks, places):
        first = pl.multiple_of(source_of(own_ref, place) * BLOCK, BLOCK)
        part = lax.dot_general(
            block[...],
            down_ref[:, pl.ds(first, BLOCK)],
            (((1,), (1,)), ((), ())),
            preferred_element_type=jnp.float32,
        )
        total = part if total is None else total + part
    return total


def weight_copies(own_ref, weight_ref, weights, done, places):
    copies = []
    for at, place in enumerate(places):
        first = pl.multiple_of(source_of(own_ref, place) * (2 * BLOCK), 2 * BLOCK)
        copies.append(
            pltpu.make_async_copy(
                weight_ref.at[pl.ds(first, 2 * BLOCK)],
                weights.at[at % BUFFERS],
                done.at[at % BUFFERS],
            )
        )
    return copies


def project_blocks(copies, blocks, weights):
    total = None
    for at, (copy, block) in enumerate(zip(copies, blocks)):
        copy.wait()
        part = jnp.dot(
            block[...],
            weights[at % BUFFERS].reshape(BLOCK, WIDE),
            preferred_element_type=jnp.float32,
        )
        total = part if total is None else total + part
        if at + BUFFERS < len(copies):
            copies[at + BUFFERS].start()
    return total


def low_begin_kernel(
    places, inverse_ref, own_ref, near_ref, far_ref, weight_ref, tokens_ref, *refs
):
    down_ref, begun_ref, up_ref, base_ref, up_rows, held, weights, done, weight_done = refs[
        len(places) - 1 :
    ]
    copies = weight_copies(own_ref, weight_ref, weights, weight_done, FIRST)
    for weight_copy in copies[:BUFFERS]:
        weight_copy.start()
    copy = pltpu.make_async_copy(tokens_ref, held, done)
    copy.start()
    core = own_ref[2]
    for shard in range(GROUPS):
        owner = inverse_ref[shard]
        rows = jnp.where(owner % 2 == core, near_ref[owner // 2], far_ref[owner // 2])
        down_ref[:, shard * 128 : (shard + 1) * 128] = rows[0:SLICE]
        rows = rows[SLICE:SENT].astype(jnp.float32)
        up_rows[2 * shard : 2 * shard + 2, :] = rows[0:2]
        up_rows[RANK + 2 * shard : RANK + 2 * shard + 2, :] = rows[2:4]
    up_ref[...] = up_rows[...].astype(jnp.bfloat16)
    copy.wait()
    blocks = [*refs[: len(places) - 1], held]
    begun_ref[...] = low_part(own_ref, blocks, down_ref, places)
    firsts = [blocks[places.index(place)] for place in FIRST]
    base_ref[...] = project_blocks(copies, firsts, weights)


def low_begin(inverse, own, near, far, weight_rows, blocks, places):
    return pl.pallas_call(
        functools.partial(low_begin_kernel, places),
        out_shape=(
            jax.ShapeDtypeStruct((SLICE, MODEL), jnp.bfloat16),
            jax.ShapeDtypeStruct((ROWS, SLICE), jnp.float32),
            pltpu.HBM((2 * RANK, HEAD), jnp.bfloat16),
            pltpu.HBM((ROWS, WIDE), jnp.float32),
        ),
        in_specs=smem(2) + vmem(2) + hbm(2) + vmem(len(places) - 1),
        out_specs=tuple(vmem(4)),
        scratch_shapes=[
            pltpu.VMEM((2 * RANK, HEAD), jnp.float32),
            pltpu.VMEM((ROWS, BLOCK), jnp.bfloat16),
            pltpu.VMEM((BUFFERS, 2 * BLOCK, HEAD), jnp.bfloat16),
            pltpu.SemaphoreType.DMA,
            pltpu.SemaphoreType.DMA((BUFFERS,)),
        ],
        compiler_params=pltpu.CompilerParams(vmem_limit_bytes=VMEM_LIMIT),
        name="low_begin",
    )(
        in_hbm(inverse),
        own,
        near,
        far,
        weight_rows,
        in_hbm(blocks[0]),
        *[blocks[place] for place in places if place],
    )


def low_end_kernel(places, own_ref, down_ref, begun_ref, *refs):
    total = begun_ref[...] + low_part(own_ref, refs[:-1], down_ref, places)
    low = total.T.astype(jnp.bfloat16)
    for target in range(SHARE):
        refs[-1][target] = low


def low_end(own, down, begun, blocks, places):
    return pl.pallas_call(
        functools.partial(low_end_kernel, places),
        out_shape=pltpu.HBM((SHARE, SLICE, ROWS), jnp.bfloat16),
        in_specs=smem(1) + vmem(2 + len(places)),
        out_specs=vmem(1)[0],
        compiler_params=pltpu.CompilerParams(vmem_limit_bytes=VMEM_LIMIT),
        name="low_end",
    )(own, down, begun, *[blocks[place] for place in places])


def project_kernel(
    places, own_ref, lengths_ref, weight_ref, up_ref, begun_ref, rate_ref, bias_ref, *refs
):
    out_ref, weights, up, begun, weight_done, done = refs[len(places) :]
    copies = weight_copies(own_ref, weight_ref, weights, weight_done, places)
    for copy in copies[:BUFFERS]:
        copy.start()
    small = [
        pltpu.make_async_copy(from_ref, to_ref, done.at[at])
        for at, (from_ref, to_ref) in enumerate(
            [(up_ref, up), (begun_ref, begun)]
        )
    ]
    for copy in small:
        copy.start()
    row = lax.broadcasted_iota(jnp.int32, (ROWS, HEAD), 0)
    begins = jnp.zeros((ROWS, HEAD), jnp.int32)
    start = jnp.int32(0)
    for piece in range(lengths_ref.shape[1]):
        begins = jnp.where(row >= start, jnp.maximum(begins, start), begins)
        start = start + lengths_ref[0, piece]
    angles = (row - begins).astype(jnp.float32) * rate_ref[...]
    low_half = lax.broadcasted_iota(jnp.int32, (ROWS, HEAD), 1) < HEAD // 2
    table = jnp.cos(jnp.where(low_half, angles, angles - np.float32(np.pi / 2)))
    swapped = pltpu.roll(table, HEAD // 2, 1)
    cosine = jnp.where(low_half, table, swapped)
    sine = jnp.where(low_half, -swapped, table)
    out_ref[:, WIDE : WIDE + HEAD] = cosine
    out_ref[:, WIDE + HEAD : 2 * WIDE] = sine
    for copy in small:
        copy.wait()
    out_ref[:, 2 * WIDE :] = up[...].astype(jnp.float32)
    total = begun[...] + project_blocks(copies, refs[: len(places)], weights)
    keys = total[:, :HEAD] + bias_ref[0:1, :].astype(jnp.float32)
    out_ref[:, :HEAD] = keys * cosine + pltpu.roll(keys, HEAD // 2, 1) * sine
    out_ref[:, HEAD:WIDE] = total[:, HEAD:] + bias_ref[1:2, :].astype(jnp.float32)


def project(own, lengths, blocks, places, weight_rows, up, begun, bias):
    half_rate = rope_base ** (-(np.arange(HEAD // 2, dtype=np.float32) * 2.0) / HEAD)
    rate = jnp.asarray(np.concatenate([half_rate, half_rate])[None], jnp.float32)
    return pl.pallas_call(
        functools.partial(project_kernel, places),
        out_shape=jax.ShapeDtypeStruct((ROWS, 2 * WIDE + HEAD), jnp.float32),
        in_specs=smem(2) + hbm(3) + vmem(len(places) + 2),
        out_specs=vmem(1)[0],
        scratch_shapes=[
            pltpu.VMEM((BUFFERS, 2 * BLOCK, HEAD), jnp.bfloat16),
            pltpu.VMEM((2 * RANK, HEAD), jnp.bfloat16),
            pltpu.VMEM((ROWS, WIDE), jnp.float32),
            pltpu.SemaphoreType.DMA((BUFFERS,)),
            pltpu.SemaphoreType.DMA((2,)),
        ],
        compiler_params=pltpu.CompilerParams(vmem_limit_bytes=VMEM_LIMIT),
        name="project",
    )(
        own,
        in_hbm(lengths),
        weight_rows,
        in_hbm(up),
        in_hbm(begun),
        in_hbm(rate),
        in_hbm(bias),
        *[blocks[place] for place in places],
    )


def finish_kernel(made_ref, low_ref, slot_ref, out_ref, placed):
    updates = []
    for side in range(2):
        ranks = slice(side * RANK, (side + 1) * RANK)
        updates.append(
            adapter_scale
            * lax.dot_general(
                low_ref[ranks, :],
                made_ref[ranks, 2 * WIDE :].astype(jnp.bfloat16),
                (((0,), (0,)), ((), ())),
                preferred_element_type=jnp.float32,
            )
        )
    keys = updates[0]
    cosine, sine = made_ref[:, WIDE : WIDE + HEAD], made_ref[:, WIDE + HEAD : 2 * WIDE]
    keys = keys * cosine + pltpu.roll(keys, HEAD // 2, 1) * sine
    rows = made_ref[:, :WIDE] + jnp.concatenate([keys, updates[1]], axis=1)
    rows = rows.astype(jnp.bfloat16)
    slots = lax.broadcasted_iota(jnp.int32, (GROUPS * CAP, ROWS), 0)
    chosen = jnp.where(slots == slot_ref[...], 1.0, 0.0).astype(jnp.bfloat16)
    slot_rows = jnp.dot(chosen, rows, preferred_element_type=jnp.float32)
    for side in range(2):
        placed[pl.ds(side, GROUPS * CAP, stride=2), :] = slot_rows[
            :, side * HEAD : (side + 1) * HEAD
        ]
    out_ref[...] = placed[...].astype(jnp.bfloat16)


def finish(made, low, slots):
    return pl.pallas_call(
        finish_kernel,
        out_shape=jax.ShapeDtypeStruct((2 * GROUPS * CAP, HEAD), jnp.bfloat16),
        in_specs=vmem(3),
        out_specs=vmem(1)[0],
        scratch_shapes=[pltpu.VMEM((2 * GROUPS * CAP, HEAD), jnp.float32)],
        compiler_params=pltpu.CompilerParams(vmem_limit_bytes=VMEM_LIMIT),
        name="finish",
    )(made, low, slots)


def slots_kernel(routes_ref, slot_ref):
    target = routes_ref[...]
    later = jnp.broadcast_to(target.astype(jnp.float32), (ROWS, ROWS))
    below = lax.broadcasted_iota(jnp.int32, (ROWS, ROWS), 0)
    after = lax.broadcasted_iota(jnp.int32, (ROWS, ROWS), 1)
    same = jnp.where((later.T == later) & (below < after), 1, 0)
    slot_ref[...] = target * CAP + jnp.sum(same, axis=0, keepdims=True)


def slots_of(routes):
    return pl.pallas_call(
        slots_kernel,
        out_shape=jax.ShapeDtypeStruct((1, ROWS), jnp.int32),
        in_specs=vmem(1),
        out_specs=vmem(1)[0],
        cost_estimate=BESIDE,
        compiler_params=pltpu.CompilerParams(vmem_limit_bytes=VMEM_LIMIT),
        name="slots",
    )(in_hbm(routes.reshape(1, ROWS)))


def body(tokens, weight, bias, down_blocks, up_blocks, lookup, lengths, routes):
    lane = lax.axis_index("tensor")
    y, x = lane // X, lane % X
    core = lax.axis_index("rollout") % 2
    own = jnp.stack([y, x, core]).astype(jnp.int32)

    weight_rows = in_hbm(weight.reshape(2 * MODEL, HEAD))

    def along_x(block, hop):
        return lax.ppermute(block, "tensor", X_HOP[hop])

    def across_y(block):
        return lax.ppermute(block, "tensor", Y_PARTNER)

    met = across_y(tokens)
    far_x, next_x, last_x = along_x(tokens, 2), along_x(tokens, 1), along_x(tokens, 3)

    sent = share(own, down_blocks.reshape(2 * 128, RANK), up_blocks.reshape(4, HEAD))
    near = lax.all_to_all(sent, "rollout", 0, 0, tiled=True, axis_index_groups=SAME_CORE)
    far = lax.ppermute(near, "rollout", SIBLING)

    slots = slots_of(routes)
    far_x, slots = lax.optimization_barrier((far_x, slots))
    met_far = across_y(far_x)
    met_next, met_last = along_x(met, 1), along_x(met, 3)
    blocks = [tokens, next_x, far_x, last_x, met, met_next, met_far, met_last]
    early, late = (1, 2, 3, 4, 0), (6, 5, 7)
    down, begun, up, started = low_begin(
        inverse_of(lookup), own, near, far, weight_rows, blocks, early
    )
    met_far, met_next, met_last, down, begun, up, started, slots = lax.optimization_barrier(
        (met_far, met_next, met_last, down, begun, up, started, slots)
    )
    blocks[5:] = [met_next, met_far, met_last]
    low = low_end(own, down, begun, blocks, late)
    low_all = lax.all_to_all(low, "tensor", 0, 0, tiled=True).reshape(2 * RANK, ROWS)
    made = project(own, lengths, blocks, REST, weight_rows, up, started, bias)
    outgoing = finish(made, low_all, slots)
    arrived = lax.all_to_all(outgoing, "rollout", 0, 0, tiled=True)
    return arrived.reshape(GROUPS * CAP, 2, HEAD)


def solution(mesh):
    in_specs = (
        P("rollout", "tensor"),
        P(None, None, "tensor"),
        P(None, "tensor"),
        P("rollout", None, None),
        P(None, "rollout", "tensor"),
        P(),
        P("rollout", None),
        P("rollout"),
    )
    out_specs = P("rollout", None, "tensor")
    return jax.shard_map(body, mesh=mesh, in_specs=in_specs, out_specs=out_specs, check_vma=False)
```

```python
import functools

import jax
import jax.numpy as jnp
import numpy as np
from jax import lax
from jax.experimental import pallas as pl
from jax.experimental.pallas import tpu as pltpu
from jax.sharding import PartitionSpec as P

HEAD = 128
GROUPS = 64
RANK = 128
MODEL = 8192
ROWS = 256
CAP = 8
X = 4

adapter_scale = 2.0
rope_base = 1000000.0

SHARE = 2 * X
WIDE = 2 * HEAD
SLICE = 2 * RANK // SHARE
SENT = SLICE + 8
BLOCK = MODEL // SHARE

SAME_CORE = [list(range(core, GROUPS, 2)) for core in range(2)]
SIBLING = [(a, a ^ 1) for a in range(GROUPS)]
X_HOP = [
    [
        (
            group * SHARE + lane // X * X + (lane + hop * (1 + 2 * (group % 2))) % X,
            group * SHARE + lane,
        )
        for group in range(GROUPS)
        for lane in range(SHARE)
    ]
    for hop in range(X)
]
Y_PARTNER = [(a, (a + X) % (2 * X)) for a in range(2 * X)]


VMEM_LIMIT = 16 * 1024 * 1024
BUFFERS = 4
FIRST = (1, 2, 0)
REST = (3, 4, 6, 5, 7)

BESIDE = pl.CostEstimate(flops=8 * 10**9, bytes_accessed=0, transcendentals=0)


def vmem(count):
    return [pl.BlockSpec(memory_space=pltpu.VMEM)] * count


def in_hbm(array):
    return pltpu.with_memory_space_constraint(array, pltpu.HBM)


def hbm(count):
    return [pl.BlockSpec(memory_space=pltpu.HBM)] * count


def smem(count):
    return [pl.BlockSpec(memory_space=pltpu.SMEM)] * count


def share_kernel(own_ref, down_ref, up_ref, out_ref, wide, turned):
    lane = own_ref[0] * X + own_ref[1]
    wide[...] = down_ref[...].astype(jnp.float32)
    turned[...] = wide[pl.ds(lane // X, 128, stride=2), :].T
    first = pl.multiple_of((lane % X) * SLICE, SLICE)
    down = turned[pl.ds(first, SLICE), :].astype(jnp.bfloat16)
    up = jnp.concatenate([up_ref[...], jnp.zeros((SENT - SLICE - 4, HEAD), jnp.bfloat16)], 0)
    sent = jnp.concatenate([down, up], 0)
    for target in range(GROUPS // 2):
        out_ref[target] = sent


def share(own, down_rows, up_rows):
    return pl.pallas_call(
        share_kernel,
        out_shape=pltpu.HBM((GROUPS // 2, SENT, HEAD), jnp.bfloat16),
        in_specs=smem(1) + vmem(2),
        out_specs=vmem(1)[0],
        scratch_shapes=[
            pltpu.VMEM((2 * 128, RANK), jnp.float32),
            pltpu.VMEM((RANK, 128), jnp.float32),
        ],
        compiler_params=pltpu.CompilerParams(vmem_limit_bytes=VMEM_LIMIT),
        name="share",
    )(own, in_hbm(down_rows), in_hbm(up_rows))


def source_of(own_ref, place):
    x = (own_ref[1] + place * (1 + 2 * own_ref[2])) % X
    return (own_ref[0] + place // X) % 2 * X + x


def inverse_kernel(lookup_ref, inverse_ref):
    for owner in range(GROUPS):
        inverse_ref[lookup_ref[owner]] = owner


def inverse_of(lookup):
    return pl.pallas_call(
        inverse_kernel,
        out_shape=pltpu.HBM((GROUPS,), jnp.int32),
        in_specs=smem(1),
        out_specs=smem(1)[0],
        cost_estimate=BESIDE,
        compiler_params=pltpu.CompilerParams(vmem_limit_bytes=VMEM_LIMIT),
        name="inverse",
    )(in_hbm(lookup))


def low_part(own_ref, blocks, down_ref, places):
    total = None
    for block, place in zip(blocks, places):
        first = pl.multiple_of(source_of(own_ref, place) * BLOCK, BLOCK)
        part = lax.dot_general(
            block[...],
            down_ref[:, pl.ds(first, BLOCK)],
            (((1,), (1,)), ((), ())),
            preferred_element_type=jnp.float32,
        )
        total = part if total is None else total + part
    return total


def weight_copies(own_ref, weight_ref, weights, done, places):
    copies = []
    for at, place in enumerate(places):
        first = pl.multiple_of(source_of(own_ref, place) * (2 * BLOCK), 2 * BLOCK)
        copies.append(
            pltpu.make_async_copy(
                weight_ref.at[pl.ds(first, 2 * BLOCK)],
                weights.at[at % BUFFERS],
                done.at[at % BUFFERS],
            )
        )
    return copies


def project_blocks(copies, blocks, weights):
    total = None
    for at, (copy, block) in enumerate(zip(copies, blocks)):
        copy.wait()
        part = jnp.dot(
            block[...],
            weights[at % BUFFERS].reshape(BLOCK, WIDE),
            preferred_element_type=jnp.float32,
        )
        total = part if total is None else total + part
        if at + BUFFERS < len(copies):
            copies[at + BUFFERS].start()
    return total


def low_begin_kernel(
    places, inverse_ref, own_ref, near_ref, far_ref, weight_ref, tokens_ref, *refs
):
    down_ref, begun_ref, up_ref, base_ref, up_rows, held, weights, done, weight_done = refs[
        len(places) - 1 :
    ]
    copies = weight_copies(own_ref, weight_ref, weights, weight_done, FIRST)
    for weight_copy in copies[:BUFFERS]:
        weight_copy.start()
    copy = pltpu.make_async_copy(tokens_ref, held, done)
    copy.start()
    core = own_ref[2]
    for shard in range(GROUPS):
        owner = inverse_ref[shard]
        rows = jnp.where(owner % 2 == core, near_ref[owner // 2], far_ref[owner // 2])
        down_ref[:, shard * 128 : (shard + 1) * 128] = rows[0:SLICE]
        rows = rows[SLICE:SENT].astype(jnp.float32)
        up_rows[2 * shard : 2 * shard + 2, :] = rows[0:2]
        up_rows[RANK + 2 * shard : RANK + 2 * shard + 2, :] = rows[2:4]
    up_ref[...] = up_rows[...].astype(jnp.bfloat16)
    copy.wait()
    blocks = [*refs[: len(places) - 1], held]
    begun_ref[...] = low_part(own_ref, blocks, down_ref, places)
    firsts = [blocks[places.index(place)] for place in FIRST]
    base_ref[...] = project_blocks(copies, firsts, weights)


def low_begin(inverse, own, near, far, weight_rows, blocks, places):
    return pl.pallas_call(
        functools.partial(low_begin_kernel, places),
        out_shape=(
            jax.ShapeDtypeStruct((SLICE, MODEL), jnp.bfloat16),
            jax.ShapeDtypeStruct((ROWS, SLICE), jnp.float32),
            pltpu.HBM((2 * RANK, HEAD), jnp.bfloat16),
            pltpu.HBM((ROWS, WIDE), jnp.float32),
        ),
        in_specs=smem(2) + vmem(2) + hbm(2) + vmem(len(places) - 1),
        out_specs=tuple(vmem(4)),
        scratch_shapes=[
            pltpu.VMEM((2 * RANK, HEAD), jnp.float32),
            pltpu.VMEM((ROWS, BLOCK), jnp.bfloat16),
            pltpu.VMEM((BUFFERS, 2 * BLOCK, HEAD), jnp.bfloat16),
            pltpu.SemaphoreType.DMA,
            pltpu.SemaphoreType.DMA((BUFFERS,)),
        ],
        compiler_params=pltpu.CompilerParams(vmem_limit_bytes=VMEM_LIMIT),
        name="low_begin",
    )(
        in_hbm(inverse),
        own,
        near,
        far,
        weight_rows,
        in_hbm(blocks[0]),
        *[blocks[place] for place in places if place],
    )


def low_end_kernel(places, own_ref, down_ref, begun_ref, *refs):
    total = begun_ref[...] + low_part(own_ref, refs[:-1], down_ref, places)
    low = total.T.astype(jnp.bfloat16)
    for target in range(SHARE):
        refs[-1][target] = low


def low_end(own, down, begun, blocks, places):
    return pl.pallas_call(
        functools.partial(low_end_kernel, places),
        out_shape=pltpu.HBM((SHARE, SLICE, ROWS), jnp.bfloat16),
        in_specs=smem(1) + vmem(2 + len(places)),
        out_specs=vmem(1)[0],
        compiler_params=pltpu.CompilerParams(vmem_limit_bytes=VMEM_LIMIT),
        name="low_end",
    )(own, down, begun, *[blocks[place] for place in places])


def project_kernel(
    places, own_ref, lengths_ref, weight_ref, up_ref, begun_ref, rate_ref, bias_ref, *refs
):
    out_ref, weights, up, begun, weight_done, done = refs[len(places) :]
    copies = weight_copies(own_ref, weight_ref, weights, weight_done, places)
    for copy in copies[:BUFFERS]:
        copy.start()
    small = [
        pltpu.make_async_copy(from_ref, to_ref, done.at[at])
        for at, (from_ref, to_ref) in enumerate(
            [(up_ref, up), (begun_ref, begun)]
        )
    ]
    for copy in small:
        copy.start()
    row = lax.broadcasted_iota(jnp.int32, (ROWS, HEAD), 0)
    begins = jnp.zeros((ROWS, HEAD), jnp.int32)
    start = jnp.int32(0)
    for piece in range(lengths_ref.shape[1]):
        begins = jnp.where(row >= start, jnp.maximum(begins, start), begins)
        start = start + lengths_ref[0, piece]
    angles = (row - begins).astype(jnp.float32) * rate_ref[...]
    low_half = lax.broadcasted_iota(jnp.int32, (ROWS, HEAD), 1) < HEAD // 2
    table = jnp.cos(jnp.where(low_half, angles, angles - np.float32(np.pi / 2)))
    swapped = pltpu.roll(table, HEAD // 2, 1)
    cosine = jnp.where(low_half, table, swapped)
    sine = jnp.where(low_half, -swapped, table)
    out_ref[:, WIDE : WIDE + HEAD] = cosine
    out_ref[:, WIDE + HEAD : 2 * WIDE] = sine
    for copy in small:
        copy.wait()
    out_ref[:, 2 * WIDE :] = up[...].astype(jnp.float32)
    total = begun[...] + project_blocks(copies, refs[: len(places)], weights)
    keys = total[:, :HEAD] + bias_ref[0:1, :].astype(jnp.float32)
    out_ref[:, :HEAD] = keys * cosine + pltpu.roll(keys, HEAD // 2, 1) * sine
    out_ref[:, HEAD:WIDE] = total[:, HEAD:] + bias_ref[1:2, :].astype(jnp.float32)


def project(own, lengths, blocks, places, weight_rows, up, begun, bias):
    half_rate = rope_base ** (-(np.arange(HEAD // 2, dtype=np.float32) * 2.0) / HEAD)
    rate = jnp.asarray(np.concatenate([half_rate, half_rate])[None], jnp.float32)
    return pl.pallas_call(
        functools.partial(project_kernel, places),
        out_shape=jax.ShapeDtypeStruct((ROWS, 2 * WIDE + HEAD), jnp.float32),
        in_specs=smem(2) + hbm(3) + vmem(len(places) + 2),
        out_specs=vmem(1)[0],
        scratch_shapes=[
            pltpu.VMEM((BUFFERS, 2 * BLOCK, HEAD), jnp.bfloat16),
            pltpu.VMEM((2 * RANK, HEAD), jnp.bfloat16),
            pltpu.VMEM((ROWS, WIDE), jnp.float32),
            pltpu.SemaphoreType.DMA((BUFFERS,)),
            pltpu.SemaphoreType.DMA((2,)),
        ],
        compiler_params=pltpu.CompilerParams(vmem_limit_bytes=VMEM_LIMIT),
        name="project",
    )(
        own,
        in_hbm(lengths),
        weight_rows,
        in_hbm(up),
        in_hbm(begun),
        in_hbm(rate),
        in_hbm(bias),
        *[blocks[place] for place in places],
    )


def finish_kernel(made_ref, low_ref, slot_ref, out_ref, placed):
    updates = []
    for side in range(2):
        ranks = slice(side * RANK, (side + 1) * RANK)
        updates.append(
            adapter_scale
            * lax.dot_general(
                low_ref[ranks, :],
                made_ref[ranks, 2 * WIDE :].astype(jnp.bfloat16),
                (((0,), (0,)), ((), ())),
                preferred_element_type=jnp.float32,
            )
        )
    keys = updates[0]
    cosine, sine = made_ref[:, WIDE : WIDE + HEAD], made_ref[:, WIDE + HEAD : 2 * WIDE]
    keys = keys * cosine + pltpu.roll(keys, HEAD // 2, 1) * sine
    rows = made_ref[:, :WIDE] + jnp.concatenate([keys, updates[1]], axis=1)
    rows = rows.astype(jnp.bfloat16)
    slots = lax.broadcasted_iota(jnp.int32, (GROUPS * CAP, ROWS), 0)
    chosen = jnp.where(slots == slot_ref[...], 1.0, 0.0).astype(jnp.bfloat16)
    slot_rows = jnp.dot(chosen, rows, preferred_element_type=jnp.float32)
    for side in range(2):
        placed[pl.ds(side, GROUPS * CAP, stride=2), :] = slot_rows[
            :, side * HEAD : (side + 1) * HEAD
        ]
    out_ref[...] = placed[...].astype(jnp.bfloat16)


def finish(made, low, slots):
    return pl.pallas_call(
        finish_kernel,
        out_shape=jax.ShapeDtypeStruct((2 * GROUPS * CAP, HEAD), jnp.bfloat16),
        in_specs=vmem(3),
        out_specs=vmem(1)[0],
        scratch_shapes=[pltpu.VMEM((2 * GROUPS * CAP, HEAD), jnp.float32)],
        compiler_params=pltpu.CompilerParams(vmem_limit_bytes=VMEM_LIMIT),
        name="finish",
    )(made, low, slots)


def slots_kernel(routes_ref, slot_ref):
    target = routes_ref[...]
    later = jnp.broadcast_to(target.astype(jnp.float32), (ROWS, ROWS))
    below = lax.broadcasted_iota(jnp.int32, (ROWS, ROWS), 0)
    after = lax.broadcasted_iota(jnp.int32, (ROWS, ROWS), 1)
    same = jnp.where((later.T == later) & (below < after), 1, 0)
    slot_ref[...] = target * CAP + jnp.sum(same, axis=0, keepdims=True)


def slots_of(routes):
    return pl.pallas_call(
        slots_kernel,
        out_shape=jax.ShapeDtypeStruct((1, ROWS), jnp.int32),
        in_specs=vmem(1),
        out_specs=vmem(1)[0],
        cost_estimate=BESIDE,
        compiler_params=pltpu.CompilerParams(vmem_limit_bytes=VMEM_LIMIT),
        name="slots",
    )(in_hbm(routes.reshape(1, ROWS)))


def body(tokens, weight, bias, down_blocks, up_blocks, lookup, lengths, routes):
    lane = lax.axis_index("tensor")
    y, x = lane // X, lane % X
    core = lax.axis_index("rollout") % 2
    own = jnp.stack([y, x, core]).astype(jnp.int32)

    weight_rows = in_hbm(weight.reshape(2 * MODEL, HEAD))

    def along_x(block, hop):
        return lax.ppermute(block, ("rollout", "tensor"), X_HOP[hop])

    def across_y(block):
        return lax.ppermute(block, "tensor", Y_PARTNER)

    met = across_y(tokens)
    far_x, next_x, last_x = along_x(tokens, 2), along_x(tokens, 1), along_x(tokens, 3)

    sent = share(own, down_blocks.reshape(2 * 128, RANK), up_blocks.reshape(4, HEAD))
    near = lax.all_to_all(sent, "rollout", 0, 0, tiled=True, axis_index_groups=SAME_CORE)
    far = lax.ppermute(near, "rollout", SIBLING)

    slots = slots_of(routes)
    far_x, slots = lax.optimization_barrier((far_x, slots))
    met_far = across_y(far_x)
    met_next, met_last = along_x(met, 1), along_x(met, 3)
    blocks = [tokens, next_x, far_x, last_x, met, met_next, met_far, met_last]
    early, late = (1, 2, 3, 4, 0), (6, 5, 7)
    down, begun, up, started = low_begin(
        inverse_of(lookup), own, near, far, weight_rows, blocks, early
    )
    met_far, met_next, met_last, down, begun, up, started, slots = lax.optimization_barrier(
        (met_far, met_next, met_last, down, begun, up, started, slots)
    )
    blocks[5:] = [met_next, met_far, met_last]
    low = low_end(own, down, begun, blocks, late)
    low_all = lax.all_to_all(low, "tensor", 0, 0, tiled=True).reshape(2 * RANK, ROWS)
    made = project(own, lengths, blocks, REST, weight_rows, up, started, bias)
    outgoing = finish(made, low_all, slots)
    arrived = lax.all_to_all(outgoing, "rollout", 0, 0, tiled=True)
    return arrived.reshape(GROUPS * CAP, 2, HEAD)


def solution(mesh):
    in_specs = (
        P("rollout", "tensor"),
        P(None, None, "tensor"),
        P(None, "tensor"),
        P("rollout", None, None),
        P(None, "rollout", "tensor"),
        P(),
        P("rollout", None),
        P("rollout"),
    )
    out_specs = P("rollout", None, "tensor")
    return jax.shard_map(body, mesh=mesh, in_specs=in_specs, out_specs=out_specs, check_vma=False)
```

```python
import functools

import jax
import jax.numpy as jnp
import numpy as np
from jax import lax
from jax.experimental import pallas as pl
from jax.experimental.pallas import tpu as pltpu
from jax.sharding import PartitionSpec as P

HEAD = 128
GROUPS = 64
RANK = 128
MODEL = 8192
ROWS = 256
CAP = 8
X = 4

adapter_scale = 2.0
rope_base = 1000000.0

SHARE = 2 * X
WIDE = 2 * HEAD
SLICE = 2 * RANK // SHARE
SENT = SLICE + 8
BLOCK = MODEL // SHARE

SAME_CORE = [list(range(core, GROUPS, 2)) for core in range(2)]
SIBLING = [(a, a ^ 1) for a in range(GROUPS)]
X_HOP = [
    [
        (
            group * SHARE + lane // X * X + (lane + hop * (1 + 2 * (group % 2))) % X,
            group * SHARE + lane,
        )
        for group in range(GROUPS)
        for lane in range(SHARE)
    ]
    for hop in range(X)
]
Y_PARTNER = [(a, (a + X) % (2 * X)) for a in range(2 * X)]


VMEM_LIMIT = 16 * 1024 * 1024
BUFFERS = 4
FIRST = (1, 2, 0)
REST = (3, 4, 6, 5, 7)

BESIDE = pl.CostEstimate(flops=8 * 10**9, bytes_accessed=0, transcendentals=0)


def vmem(count):
    return [pl.BlockSpec(memory_space=pltpu.VMEM)] * count


def in_hbm(array):
    return pltpu.with_memory_space_constraint(array, pltpu.HBM)


def hbm(count):
    return [pl.BlockSpec(memory_space=pltpu.HBM)] * count


def smem(count):
    return [pl.BlockSpec(memory_space=pltpu.SMEM)] * count


def share_kernel(own_ref, down_ref, up_ref, out_ref, wide, turned):
    lane = own_ref[0] * X + own_ref[1]
    wide[...] = down_ref[...].astype(jnp.float32)
    turned[...] = wide[pl.ds(lane // X, 128, stride=2), :].T
    first = pl.multiple_of((lane % X) * SLICE, SLICE)
    down = turned[pl.ds(first, SLICE), :].astype(jnp.bfloat16)
    up = jnp.concatenate([up_ref[...], jnp.zeros((SENT - SLICE - 4, HEAD), jnp.bfloat16)], 0)
    sent = jnp.concatenate([down, up], 0)
    for target in range(GROUPS // 2):
        out_ref[target] = sent


def share(own, down_rows, up_rows):
    return pl.pallas_call(
        share_kernel,
        out_shape=pltpu.HBM((GROUPS // 2, SENT, HEAD), jnp.bfloat16),
        in_specs=smem(1) + vmem(2),
        out_specs=vmem(1)[0],
        scratch_shapes=[
            pltpu.VMEM((2 * 128, RANK), jnp.float32),
            pltpu.VMEM((RANK, 128), jnp.float32),
        ],
        compiler_params=pltpu.CompilerParams(vmem_limit_bytes=VMEM_LIMIT),
        name="share",
    )(own, in_hbm(down_rows), in_hbm(up_rows))


def source_of(own_ref, place):
    x = (own_ref[1] + place * (1 + 2 * own_ref[2])) % X
    return (own_ref[0] + place // X) % 2 * X + x


def places_kernel(lookup_ref, routes_ref, inverse_ref, slot_ref):
    for owner in range(GROUPS):
        inverse_ref[lookup_ref[owner]] = owner
    target = routes_ref[...]
    later = jnp.broadcast_to(target.astype(jnp.float32), (ROWS, ROWS))
    below = lax.broadcasted_iota(jnp.int32, (ROWS, ROWS), 0)
    after = lax.broadcasted_iota(jnp.int32, (ROWS, ROWS), 1)
    same = jnp.where((later.T == later) & (below < after), 1, 0)
    slot_ref[...] = target * CAP + jnp.sum(same, axis=0, keepdims=True)


def places_of(lookup, routes):
    return pl.pallas_call(
        places_kernel,
        out_shape=(
            pltpu.HBM((GROUPS,), jnp.int32),
            jax.ShapeDtypeStruct((1, ROWS), jnp.int32),
        ),
        in_specs=smem(1) + vmem(1),
        out_specs=(smem(1)[0], vmem(1)[0]),
        cost_estimate=BESIDE,
        compiler_params=pltpu.CompilerParams(vmem_limit_bytes=VMEM_LIMIT),
        name="places",
    )(in_hbm(lookup), in_hbm(routes.reshape(1, ROWS)))


def low_part(own_ref, blocks, down_ref, places):
    total = None
    for block, place in zip(blocks, places):
        first = pl.multiple_of(source_of(own_ref, place) * BLOCK, BLOCK)
        part = lax.dot_general(
            block[...],
            down_ref[:, pl.ds(first, BLOCK)],
            (((1,), (1,)), ((), ())),
            preferred_element_type=jnp.float32,
        )
        total = part if total is None else total + part
    return total


def weight_copies(own_ref, weight_ref, weights, done, places):
    copies = []
    for at, place in enumerate(places):
        first = pl.multiple_of(source_of(own_ref, place) * (2 * BLOCK), 2 * BLOCK)
        copies.append(
            pltpu.make_async_copy(
                weight_ref.at[pl.ds(first, 2 * BLOCK)],
                weights.at[at % BUFFERS],
                done.at[at % BUFFERS],
            )
        )
    return copies


def project_blocks(copies, blocks, weights):
    total = None
    for at, (copy, block) in enumerate(zip(copies, blocks)):
        copy.wait()
        part = jnp.dot(
            block[...],
            weights[at % BUFFERS].reshape(BLOCK, WIDE),
            preferred_element_type=jnp.float32,
        )
        total = part if total is None else total + part
        if at + BUFFERS < len(copies):
            copies[at + BUFFERS].start()
    return total


def low_begin_kernel(
    places, inverse_ref, own_ref, near_ref, far_ref, weight_ref, tokens_ref, *refs
):
    down_ref, begun_ref, up_ref, base_ref, up_rows, held, weights, done, weight_done = refs[
        len(places) - 1 :
    ]
    copies = weight_copies(own_ref, weight_ref, weights, weight_done, FIRST)
    for weight_copy in copies[:BUFFERS]:
        weight_copy.start()
    copy = pltpu.make_async_copy(tokens_ref, held, done)
    copy.start()
    core = own_ref[2]
    for shard in range(GROUPS):
        owner = inverse_ref[shard]
        rows = jnp.where(owner % 2 == core, near_ref[owner // 2], far_ref[owner // 2])
        down_ref[:, shard * 128 : (shard + 1) * 128] = rows[0:SLICE]
        rows = rows[SLICE:SENT].astype(jnp.float32)
        up_rows[2 * shard : 2 * shard + 2, :] = rows[0:2]
        up_rows[RANK + 2 * shard : RANK + 2 * shard + 2, :] = rows[2:4]
    up_ref[...] = up_rows[...].astype(jnp.bfloat16)
    copy.wait()
    blocks = [*refs[: len(places) - 1], held]
    begun_ref[...] = low_part(own_ref, blocks, down_ref, places)
    firsts = [blocks[places.index(place)] for place in FIRST]
    base_ref[...] = project_blocks(copies, firsts, weights)


def low_begin(inverse, own, near, far, weight_rows, blocks, places):
    return pl.pallas_call(
        functools.partial(low_begin_kernel, places),
        out_shape=(
            jax.ShapeDtypeStruct((SLICE, MODEL), jnp.bfloat16),
            jax.ShapeDtypeStruct((ROWS, SLICE), jnp.float32),
            pltpu.HBM((2 * RANK, HEAD), jnp.bfloat16),
            pltpu.HBM((ROWS, WIDE), jnp.float32),
        ),
        in_specs=smem(2) + vmem(2) + hbm(2) + vmem(len(places) - 1),
        out_specs=tuple(vmem(4)),
        scratch_shapes=[
            pltpu.VMEM((2 * RANK, HEAD), jnp.float32),
            pltpu.VMEM((ROWS, BLOCK), jnp.bfloat16),
            pltpu.VMEM((BUFFERS, 2 * BLOCK, HEAD), jnp.bfloat16),
            pltpu.SemaphoreType.DMA,
            pltpu.SemaphoreType.DMA((BUFFERS,)),
        ],
        compiler_params=pltpu.CompilerParams(vmem_limit_bytes=VMEM_LIMIT),
        name="low_begin",
    )(
        in_hbm(inverse),
        own,
        near,
        far,
        weight_rows,
        in_hbm(blocks[0]),
        *[blocks[place] for place in places if place],
    )


def low_end_kernel(places, own_ref, down_ref, begun_ref, *refs):
    total = begun_ref[...] + low_part(own_ref, refs[:-1], down_ref, places)
    low = total.T.astype(jnp.bfloat16)
    for target in range(SHARE):
        refs[-1][target] = low


def low_end(own, down, begun, blocks, places):
    return pl.pallas_call(
        functools.partial(low_end_kernel, places),
        out_shape=pltpu.HBM((SHARE, SLICE, ROWS), jnp.bfloat16),
        in_specs=smem(1) + vmem(2 + len(places)),
        out_specs=vmem(1)[0],
        compiler_params=pltpu.CompilerParams(vmem_limit_bytes=VMEM_LIMIT),
        name="low_end",
    )(own, down, begun, *[blocks[place] for place in places])


def project_kernel(
    places, own_ref, lengths_ref, weight_ref, up_ref, begun_ref, rate_ref, bias_ref, *refs
):
    out_ref, weights, up, begun, weight_done, done = refs[len(places) :]
    copies = weight_copies(own_ref, weight_ref, weights, weight_done, places)
    for copy in copies[:BUFFERS]:
        copy.start()
    small = [
        pltpu.make_async_copy(from_ref, to_ref, done.at[at])
        for at, (from_ref, to_ref) in enumerate(
            [(up_ref, up), (begun_ref, begun)]
        )
    ]
    for copy in small:
        copy.start()
    row = lax.broadcasted_iota(jnp.int32, (ROWS, HEAD), 0)
    begins = jnp.zeros((ROWS, HEAD), jnp.int32)
    start = jnp.int32(0)
    for piece in range(lengths_ref.shape[1]):
        begins = jnp.where(row >= start, jnp.maximum(begins, start), begins)
        start = start + lengths_ref[0, piece]
    angles = (row - begins).astype(jnp.float32) * rate_ref[...]
    low_half = lax.broadcasted_iota(jnp.int32, (ROWS, HEAD), 1) < HEAD // 2
    table = jnp.cos(jnp.where(low_half, angles, angles - np.float32(np.pi / 2)))
    swapped = pltpu.roll(table, HEAD // 2, 1)
    cosine = jnp.where(low_half, table, swapped)
    sine = jnp.where(low_half, -swapped, table)
    out_ref[:, WIDE : WIDE + HEAD] = cosine
    out_ref[:, WIDE + HEAD : 2 * WIDE] = sine
    for copy in small:
        copy.wait()
    out_ref[:, 2 * WIDE :] = up[...].astype(jnp.float32)
    total = begun[...] + project_blocks(copies, refs[: len(places)], weights)
    keys = total[:, :HEAD] + bias_ref[0:1, :].astype(jnp.float32)
    out_ref[:, :HEAD] = keys * cosine + pltpu.roll(keys, HEAD // 2, 1) * sine
    out_ref[:, HEAD:WIDE] = total[:, HEAD:] + bias_ref[1:2, :].astype(jnp.float32)


def project(own, lengths, rate, blocks, places, weight_rows, up, begun, bias):
    return pl.pallas_call(
        functools.partial(project_kernel, places),
        out_shape=jax.ShapeDtypeStruct((ROWS, 2 * WIDE + HEAD), jnp.float32),
        in_specs=smem(2) + hbm(3) + vmem(len(places) + 2),
        out_specs=vmem(1)[0],
        scratch_shapes=[
            pltpu.VMEM((BUFFERS, 2 * BLOCK, HEAD), jnp.bfloat16),
            pltpu.VMEM((2 * RANK, HEAD), jnp.bfloat16),
            pltpu.VMEM((ROWS, WIDE), jnp.float32),
            pltpu.SemaphoreType.DMA((BUFFERS,)),
            pltpu.SemaphoreType.DMA((2,)),
        ],
        compiler_params=pltpu.CompilerParams(vmem_limit_bytes=VMEM_LIMIT),
        name="project",
    )(
        own,
        in_hbm(lengths),
        weight_rows,
        in_hbm(up),
        in_hbm(begun),
        in_hbm(rate),
        in_hbm(bias),
        *[blocks[place] for place in places],
    )


def finish_kernel(made_ref, low_ref, slot_ref, out_ref, placed):
    updates = []
    for side in range(2):
        ranks = slice(side * RANK, (side + 1) * RANK)
        updates.append(
            adapter_scale
            * lax.dot_general(
                low_ref[ranks, :],
                made_ref[ranks, 2 * WIDE :].astype(jnp.bfloat16),
                (((0,), (0,)), ((), ())),
                preferred_element_type=jnp.float32,
            )
        )
    keys = updates[0]
    cosine, sine = made_ref[:, WIDE : WIDE + HEAD], made_ref[:, WIDE + HEAD : 2 * WIDE]
    keys = keys * cosine + pltpu.roll(keys, HEAD // 2, 1) * sine
    rows = made_ref[:, :WIDE] + jnp.concatenate([keys, updates[1]], axis=1)
    rows = rows.astype(jnp.bfloat16)
    slots = lax.broadcasted_iota(jnp.int32, (GROUPS * CAP, ROWS), 0)
    chosen = jnp.where(slots == slot_ref[...], 1.0, 0.0).astype(jnp.bfloat16)
    slot_rows = jnp.dot(chosen, rows, preferred_element_type=jnp.float32)
    for side in range(2):
        placed[pl.ds(side, GROUPS * CAP, stride=2), :] = slot_rows[
            :, side * HEAD : (side + 1) * HEAD
        ]
    out_ref[...] = placed[...].astype(jnp.bfloat16)


def finish(made, low, slots):
    return pl.pallas_call(
        finish_kernel,
        out_shape=jax.ShapeDtypeStruct((2 * GROUPS * CAP, HEAD), jnp.bfloat16),
        in_specs=vmem(3),
        out_specs=vmem(1)[0],
        scratch_shapes=[pltpu.VMEM((2 * GROUPS * CAP, HEAD), jnp.float32)],
        compiler_params=pltpu.CompilerParams(vmem_limit_bytes=VMEM_LIMIT),
        name="finish",
    )(made, low, slots)


def rate_kernel(rate_ref):
    lane = lax.broadcasted_iota(jnp.int32, (1, HEAD), 1) % (HEAD // 2)
    rate_ref[...] = jnp.exp(lane.astype(jnp.float32) * np.float32(-2.0 * np.log(rope_base) / HEAD))


def rates():
    return pl.pallas_call(
        rate_kernel,
        out_shape=pltpu.HBM((1, HEAD), jnp.float32),
        in_specs=[],
        out_specs=vmem(1)[0],
        cost_estimate=BESIDE,
        compiler_params=pltpu.CompilerParams(vmem_limit_bytes=VMEM_LIMIT),
        name="rate",
    )()


def body(tokens, weight, bias, down_blocks, up_blocks, lookup, lengths, routes):
    lane = lax.axis_index("tensor")
    y, x = lane // X, lane % X
    core = lax.axis_index("rollout") % 2
    own = jnp.stack([y, x, core]).astype(jnp.int32)

    weight_rows = in_hbm(weight.reshape(2 * MODEL, HEAD))

    def along_x(block, hop):
        return lax.ppermute(block, ("rollout", "tensor"), X_HOP[hop])

    def across_y(block):
        return lax.ppermute(block, "tensor", Y_PARTNER)

    met = across_y(tokens)
    far_x, next_x, last_x = along_x(tokens, 2), along_x(tokens, 1), along_x(tokens, 3)

    sent = share(own, down_blocks.reshape(2 * 128, RANK), up_blocks.reshape(4, HEAD))
    near = lax.all_to_all(sent, "rollout", 0, 0, tiled=True, axis_index_groups=SAME_CORE)
    far = lax.ppermute(near, "rollout", SIBLING)

    rate = rates()
    far_x, rate = lax.optimization_barrier((far_x, rate))
    inverse, slots = places_of(lookup, routes)
    met_far = across_y(far_x)
    met_next, met_last = along_x(met, 1), along_x(met, 3)
    blocks = [tokens, next_x, far_x, last_x, met, met_next, met_far, met_last]
    early, late = (1, 2, 3, 4, 0), (6, 5, 7)
    down, begun, up, started = low_begin(
        inverse, own, near, far, weight_rows, blocks, early
    )
    met_far, met_next, met_last, down, begun, up, started, slots = lax.optimization_barrier(
        (met_far, met_next, met_last, down, begun, up, started, slots)
    )
    blocks[5:] = [met_next, met_far, met_last]
    low = low_end(own, down, begun, blocks, late)
    low_all = lax.all_to_all(low, "tensor", 0, 0, tiled=True).reshape(2 * RANK, ROWS)
    made = project(own, lengths, rate, blocks, REST, weight_rows, up, started, bias)
    outgoing = finish(made, low_all, slots)
    arrived = lax.all_to_all(outgoing, "rollout", 0, 0, tiled=True)
    return arrived.reshape(GROUPS * CAP, 2, HEAD)


def solution(mesh):
    in_specs = (
        P("rollout", "tensor"),
        P(None, None, "tensor"),
        P(None, "tensor"),
        P("rollout", None, None),
        P(None, "rollout", "tensor"),
        P(),
        P("rollout", None),
        P("rollout"),
    )
    out_specs = P("rollout", None, "tensor")
    return jax.shard_map(body, mesh=mesh, in_specs=in_specs, out_specs=out_specs, check_vma=False)
```

```python
import functools

import jax
import jax.numpy as jnp
import numpy as np
from jax import lax
from jax.experimental import pallas as pl
from jax.experimental.pallas import tpu as pltpu
from jax.sharding import PartitionSpec as P

HEAD = 128
GROUPS = 64
RANK = 128
MODEL = 8192
ROWS = 256
CAP = 8
X = 4

adapter_scale = 2.0
rope_base = 1000000.0

SHARE = 2 * X
WIDE = 2 * HEAD
SLICE = 2 * RANK // SHARE
SENT = SLICE + 8
BLOCK = MODEL // SHARE

SAME_CORE = [list(range(core, GROUPS, 2)) for core in range(2)]
SIBLING = [(a, a ^ 1) for a in range(GROUPS)]
X_HOP = [
    [
        (
            group * SHARE + lane // X * X + (lane + hop * (1 + 2 * (group % 2))) % X,
            group * SHARE + lane,
        )
        for group in range(GROUPS)
        for lane in range(SHARE)
    ]
    for hop in range(X)
]
Y_PARTNER = [(a, (a + X) % (2 * X)) for a in range(2 * X)]


VMEM_LIMIT = 16 * 1024 * 1024
BUFFERS = 5
FIRST = (1, 2, 0)
REST = (3, 4, 6, 5, 7)

BESIDE = pl.CostEstimate(flops=8 * 10**9, bytes_accessed=0, transcendentals=0)


def vmem(count):
    return [pl.BlockSpec(memory_space=pltpu.VMEM)] * count


def in_hbm(array):
    return pltpu.with_memory_space_constraint(array, pltpu.HBM)


def hbm(count):
    return [pl.BlockSpec(memory_space=pltpu.HBM)] * count


def smem(count):
    return [pl.BlockSpec(memory_space=pltpu.SMEM)] * count


def share_kernel(own_ref, down_ref, up_ref, out_ref, wide, turned):
    lane = own_ref[0] * X + own_ref[1]
    wide[...] = down_ref[...].astype(jnp.float32)
    turned[...] = wide[pl.ds(lane // X, 128, stride=2), :].T
    first = pl.multiple_of((lane % X) * SLICE, SLICE)
    down = turned[pl.ds(first, SLICE), :].astype(jnp.bfloat16)
    up = jnp.concatenate([up_ref[...], jnp.zeros((SENT - SLICE - 4, HEAD), jnp.bfloat16)], 0)
    sent = jnp.concatenate([down, up], 0)
    for target in range(GROUPS // 2):
        out_ref[target] = sent


def share(own, down_rows, up_rows):
    return pl.pallas_call(
        share_kernel,
        out_shape=pltpu.HBM((GROUPS // 2, SENT, HEAD), jnp.bfloat16),
        in_specs=smem(1) + vmem(2),
        out_specs=vmem(1)[0],
        scratch_shapes=[
            pltpu.VMEM((2 * 128, RANK), jnp.float32),
            pltpu.VMEM((RANK, 128), jnp.float32),
        ],
        compiler_params=pltpu.CompilerParams(vmem_limit_bytes=VMEM_LIMIT),
        name="share",
    )(own, in_hbm(down_rows), in_hbm(up_rows))


def source_of(own_ref, place):
    x = (own_ref[1] + place * (1 + 2 * own_ref[2])) % X
    return (own_ref[0] + place // X) % 2 * X + x


def places_kernel(lookup_ref, routes_ref, inverse_ref, slot_ref):
    for owner in range(GROUPS):
        inverse_ref[lookup_ref[owner]] = owner
    target = routes_ref[...]
    later = jnp.broadcast_to(target.astype(jnp.float32), (ROWS, ROWS))
    below = lax.broadcasted_iota(jnp.int32, (ROWS, ROWS), 0)
    after = lax.broadcasted_iota(jnp.int32, (ROWS, ROWS), 1)
    same = jnp.where((later.T == later) & (below < after), 1, 0)
    slot_ref[...] = target * CAP + jnp.sum(same, axis=0, keepdims=True)


def places_of(lookup, routes):
    return pl.pallas_call(
        places_kernel,
        out_shape=(
            pltpu.HBM((GROUPS,), jnp.int32),
            jax.ShapeDtypeStruct((1, ROWS), jnp.int32),
        ),
        in_specs=smem(1) + vmem(1),
        out_specs=(smem(1)[0], vmem(1)[0]),
        cost_estimate=BESIDE,
        compiler_params=pltpu.CompilerParams(vmem_limit_bytes=VMEM_LIMIT),
        name="places",
    )(in_hbm(lookup), in_hbm(routes.reshape(1, ROWS)))


def low_part(own_ref, blocks, down_ref, places):
    total = None
    for block, place in zip(blocks, places):
        first = pl.multiple_of(source_of(own_ref, place) * BLOCK, BLOCK)
        part = lax.dot_general(
            block[...],
            down_ref[:, pl.ds(first, BLOCK)],
            (((1,), (1,)), ((), ())),
            preferred_element_type=jnp.float32,
        )
        total = part if total is None else total + part
    return total


def weight_copies(own_ref, weight_ref, weights, done, places):
    copies = []
    for at, place in enumerate(places):
        first = pl.multiple_of(source_of(own_ref, place) * (2 * BLOCK), 2 * BLOCK)
        copies.append(
            pltpu.make_async_copy(
                weight_ref.at[pl.ds(first, 2 * BLOCK)],
                weights.at[at % BUFFERS],
                done.at[at % BUFFERS],
            )
        )
    return copies


def project_blocks(copies, blocks, weights):
    total = None
    for at, (copy, block) in enumerate(zip(copies, blocks)):
        copy.wait()
        part = jnp.dot(
            block[...],
            weights[at % BUFFERS].reshape(BLOCK, WIDE),
            preferred_element_type=jnp.float32,
        )
        total = part if total is None else total + part
        if at + BUFFERS < len(copies):
            copies[at + BUFFERS].start()
    return total


def low_begin_kernel(
    places, inverse_ref, own_ref, near_ref, far_ref, weight_ref, tokens_ref, *refs
):
    down_ref, begun_ref, up_ref, base_ref, up_rows, held, weights, done, weight_done = refs[
        len(places) - 1 :
    ]
    copies = weight_copies(own_ref, weight_ref, weights, weight_done, FIRST)
    for weight_copy in copies[:BUFFERS]:
        weight_copy.start()
    copy = pltpu.make_async_copy(tokens_ref, held, done)
    copy.start()
    core = own_ref[2]
    for shard in range(GROUPS):
        owner = inverse_ref[shard]
        rows = jnp.where(owner % 2 == core, near_ref[owner // 2], far_ref[owner // 2])
        down_ref[:, shard * 128 : (shard + 1) * 128] = rows[0:SLICE]
        rows = rows[SLICE:SENT].astype(jnp.float32)
        up_rows[2 * shard : 2 * shard + 2, :] = rows[0:2]
        up_rows[RANK + 2 * shard : RANK + 2 * shard + 2, :] = rows[2:4]
    up_ref[...] = up_rows[...].astype(jnp.bfloat16)
    copy.wait()
    blocks = [*refs[: len(places) - 1], held]
    begun_ref[...] = low_part(own_ref, blocks, down_ref, places)
    firsts = [blocks[places.index(place)] for place in FIRST]
    base_ref[...] = project_blocks(copies, firsts, weights)


def low_begin(inverse, own, near, far, weight_rows, blocks, places):
    return pl.pallas_call(
        functools.partial(low_begin_kernel, places),
        out_shape=(
            jax.ShapeDtypeStruct((SLICE, MODEL), jnp.bfloat16),
            jax.ShapeDtypeStruct((ROWS, SLICE), jnp.float32),
            pltpu.HBM((2 * RANK, HEAD), jnp.bfloat16),
            pltpu.HBM((ROWS, WIDE), jnp.float32),
        ),
        in_specs=smem(2) + vmem(2) + hbm(2) + vmem(len(places) - 1),
        out_specs=tuple(vmem(4)),
        scratch_shapes=[
            pltpu.VMEM((2 * RANK, HEAD), jnp.float32),
            pltpu.VMEM((ROWS, BLOCK), jnp.bfloat16),
            pltpu.VMEM((len(FIRST), 2 * BLOCK, HEAD), jnp.bfloat16),
            pltpu.SemaphoreType.DMA,
            pltpu.SemaphoreType.DMA((len(FIRST),)),
        ],
        compiler_params=pltpu.CompilerParams(vmem_limit_bytes=VMEM_LIMIT),
        name="low_begin",
    )(
        in_hbm(inverse),
        own,
        near,
        far,
        weight_rows,
        in_hbm(blocks[0]),
        *[blocks[place] for place in places if place],
    )


def low_end_kernel(places, own_ref, down_ref, begun_ref, *refs):
    total = begun_ref[...] + low_part(own_ref, refs[:-1], down_ref, places)
    low = total.T.astype(jnp.bfloat16)
    for target in range(SHARE):
        refs[-1][target] = low


def low_end(own, down, begun, blocks, places):
    return pl.pallas_call(
        functools.partial(low_end_kernel, places),
        out_shape=pltpu.HBM((SHARE, SLICE, ROWS), jnp.bfloat16),
        in_specs=smem(1) + vmem(2 + len(places)),
        out_specs=vmem(1)[0],
        compiler_params=pltpu.CompilerParams(vmem_limit_bytes=VMEM_LIMIT),
        name="low_end",
    )(own, down, begun, *[blocks[place] for place in places])


def project_kernel(
    places, own_ref, lengths_ref, weight_ref, up_ref, begun_ref, rate_ref, bias_ref, *refs
):
    out_ref, weights, up, begun, weight_done, done = refs[len(places) :]
    copies = weight_copies(own_ref, weight_ref, weights, weight_done, places)
    for copy in copies[:BUFFERS]:
        copy.start()
    small = [
        pltpu.make_async_copy(from_ref, to_ref, done.at[at])
        for at, (from_ref, to_ref) in enumerate(
            [(up_ref, up), (begun_ref, begun)]
        )
    ]
    for copy in small:
        copy.start()
    row = lax.broadcasted_iota(jnp.int32, (ROWS, HEAD), 0)
    begins = jnp.zeros((ROWS, HEAD), jnp.int32)
    start = jnp.int32(0)
    for piece in range(lengths_ref.shape[1]):
        begins = jnp.where(row >= start, jnp.maximum(begins, start), begins)
        start = start + lengths_ref[0, piece]
    angles = (row - begins).astype(jnp.float32) * rate_ref[...]
    low_half = lax.broadcasted_iota(jnp.int32, (ROWS, HEAD), 1) < HEAD // 2
    table = jnp.cos(jnp.where(low_half, angles, angles - np.float32(np.pi / 2)))
    swapped = pltpu.roll(table, HEAD // 2, 1)
    cosine = jnp.where(low_half, table, swapped)
    sine = jnp.where(low_half, -swapped, table)
    out_ref[:, WIDE : WIDE + HEAD] = cosine
    out_ref[:, WIDE + HEAD : 2 * WIDE] = sine
    for copy in small:
        copy.wait()
    out_ref[:, 2 * WIDE :] = up[...].astype(jnp.float32)
    total = begun[...] + project_blocks(copies, refs[: len(places)], weights)
    keys = total[:, :HEAD] + bias_ref[0:1, :].astype(jnp.float32)
    out_ref[:, :HEAD] = keys * cosine + pltpu.roll(keys, HEAD // 2, 1) * sine
    out_ref[:, HEAD:WIDE] = total[:, HEAD:] + bias_ref[1:2, :].astype(jnp.float32)


def project(own, lengths, rate, blocks, places, weight_rows, up, begun, bias):
    return pl.pallas_call(
        functools.partial(project_kernel, places),
        out_shape=jax.ShapeDtypeStruct((ROWS, 2 * WIDE + HEAD), jnp.float32),
        in_specs=smem(2) + hbm(3) + vmem(len(places) + 2),
        out_specs=vmem(1)[0],
        scratch_shapes=[
            pltpu.VMEM((BUFFERS, 2 * BLOCK, HEAD), jnp.bfloat16),
            pltpu.VMEM((2 * RANK, HEAD), jnp.bfloat16),
            pltpu.VMEM((ROWS, WIDE), jnp.float32),
            pltpu.SemaphoreType.DMA((BUFFERS,)),
            pltpu.SemaphoreType.DMA((2,)),
        ],
        compiler_params=pltpu.CompilerParams(vmem_limit_bytes=VMEM_LIMIT),
        name="project",
    )(
        own,
        in_hbm(lengths),
        weight_rows,
        in_hbm(up),
        in_hbm(begun),
        in_hbm(rate),
        in_hbm(bias),
        *[blocks[place] for place in places],
    )


def finish_kernel(made_ref, low_ref, slot_ref, out_ref, placed):
    updates = []
    for side in range(2):
        ranks = slice(side * RANK, (side + 1) * RANK)
        updates.append(
            adapter_scale
            * lax.dot_general(
                low_ref[ranks, :],
                made_ref[ranks, 2 * WIDE :].astype(jnp.bfloat16),
                (((0,), (0,)), ((), ())),
                preferred_element_type=jnp.float32,
            )
        )
    keys = updates[0]
    cosine, sine = made_ref[:, WIDE : WIDE + HEAD], made_ref[:, WIDE + HEAD : 2 * WIDE]
    keys = keys * cosine + pltpu.roll(keys, HEAD // 2, 1) * sine
    rows = made_ref[:, :WIDE] + jnp.concatenate([keys, updates[1]], axis=1)
    rows = rows.astype(jnp.bfloat16)
    slots = lax.broadcasted_iota(jnp.int32, (GROUPS * CAP, ROWS), 0)
    chosen = jnp.where(slots == slot_ref[...], 1.0, 0.0).astype(jnp.bfloat16)
    slot_rows = jnp.dot(chosen, rows, preferred_element_type=jnp.float32)
    for side in range(2):
        placed[pl.ds(side, GROUPS * CAP, stride=2), :] = slot_rows[
            :, side * HEAD : (side + 1) * HEAD
        ]
    out_ref[...] = placed[...].astype(jnp.bfloat16)


def finish(made, low, slots):
    return pl.pallas_call(
        finish_kernel,
        out_shape=jax.ShapeDtypeStruct((2 * GROUPS * CAP, HEAD), jnp.bfloat16),
        in_specs=vmem(3),
        out_specs=vmem(1)[0],
        scratch_shapes=[pltpu.VMEM((2 * GROUPS * CAP, HEAD), jnp.float32)],
        compiler_params=pltpu.CompilerParams(vmem_limit_bytes=VMEM_LIMIT),
        name="finish",
    )(made, low, slots)


def rate_kernel(rate_ref):
    lane = lax.broadcasted_iota(jnp.int32, (1, HEAD), 1) % (HEAD // 2)
    rate_ref[...] = jnp.exp(lane.astype(jnp.float32) * np.float32(-2.0 * np.log(rope_base) / HEAD))


def rates():
    return pl.pallas_call(
        rate_kernel,
        out_shape=pltpu.HBM((1, HEAD), jnp.float32),
        in_specs=[],
        out_specs=vmem(1)[0],
        cost_estimate=BESIDE,
        compiler_params=pltpu.CompilerParams(vmem_limit_bytes=VMEM_LIMIT),
        name="rate",
    )()


def body(tokens, weight, bias, down_blocks, up_blocks, lookup, lengths, routes):
    lane = lax.axis_index("tensor")
    y, x = lane // X, lane % X
    core = lax.axis_index("rollout") % 2
    own = jnp.stack([y, x, core]).astype(jnp.int32)

    weight_rows = in_hbm(weight.reshape(2 * MODEL, HEAD))

    def along_x(block, hop):
        return lax.ppermute(block, ("rollout", "tensor"), X_HOP[hop])

    def across_y(block):
        return lax.ppermute(block, "tensor", Y_PARTNER)

    met = across_y(tokens)
    far_x, next_x, last_x = along_x(tokens, 2), along_x(tokens, 1), along_x(tokens, 3)

    sent = share(own, down_blocks.reshape(2 * 128, RANK), up_blocks.reshape(4, HEAD))
    near = lax.all_to_all(sent, "rollout", 0, 0, tiled=True, axis_index_groups=SAME_CORE)
    far = lax.ppermute(near, "rollout", SIBLING)

    rate = rates()
    far_x, rate = lax.optimization_barrier((far_x, rate))
    inverse, slots = places_of(lookup, routes)
    met_far = across_y(far_x)
    met_next, met_last = along_x(met, 1), along_x(met, 3)
    blocks = [tokens, next_x, far_x, last_x, met, met_next, met_far, met_last]
    early, late = (1, 2, 3, 4, 0), (6, 5, 7)
    down, begun, up, started = low_begin(
        inverse, own, near, far, weight_rows, blocks, early
    )
    met_far, met_next, met_last, down, begun, up, started, slots = lax.optimization_barrier(
        (met_far, met_next, met_last, down, begun, up, started, slots)
    )
    blocks[5:] = [met_next, met_far, met_last]
    low = low_end(own, down, begun, blocks, late)
    low_all = lax.all_to_all(low, "tensor", 0, 0, tiled=True).reshape(2 * RANK, ROWS)
    made = project(own, lengths, rate, blocks, REST, weight_rows, up, started, bias)
    outgoing = finish(made, low_all, slots)
    arrived = lax.all_to_all(outgoing, "rollout", 0, 0, tiled=True)
    return arrived.reshape(GROUPS * CAP, 2, HEAD)


def solution(mesh):
    in_specs = (
        P("rollout", "tensor"),
        P(None, None, "tensor"),
        P(None, "tensor"),
        P("rollout", None, None),
        P(None, "rollout", "tensor"),
        P(),
        P("rollout", None),
        P("rollout"),
    )
    out_specs = P("rollout", None, "tensor")
    return jax.shard_map(body, mesh=mesh, in_specs=in_specs, out_specs=out_specs, check_vma=False)
```

```python
import functools

import jax
import jax.numpy as jnp
import numpy as np
from jax import lax
from jax.experimental import pallas as pl
from jax.experimental.pallas import tpu as pltpu
from jax.sharding import PartitionSpec as P

HEAD = 128
GROUPS = 64
RANK = 128
MODEL = 8192
ROWS = 256
CAP = 8
X = 4

adapter_scale = 2.0
rope_base = 1000000.0

SHARE = 2 * X
WIDE = 2 * HEAD
SLICE = 2 * RANK // SHARE
SENT = SLICE + 8
BLOCK = MODEL // SHARE

SAME_CORE = [list(range(core, GROUPS, 2)) for core in range(2)]
SIBLING = [(a, a ^ 1) for a in range(GROUPS)]
X_HOP = [
    [
        (
            group * SHARE + lane // X * X + (lane + hop * (1 + 2 * (group % 2))) % X,
            group * SHARE + lane,
        )
        for group in range(GROUPS)
        for lane in range(SHARE)
    ]
    for hop in range(X)
]
Y_PARTNER = [(a, (a + X) % (2 * X)) for a in range(2 * X)]


VMEM_LIMIT = 16 * 1024 * 1024
BUFFERS = 5
FIRST = (1, 2, 0)
REST = (3, 4, 6, 5, 7)

BESIDE = pl.CostEstimate(flops=8 * 10**9, bytes_accessed=0, transcendentals=0)


def vmem(count):
    return [pl.BlockSpec(memory_space=pltpu.VMEM)] * count


def in_hbm(array):
    return pltpu.with_memory_space_constraint(array, pltpu.HBM)


def hbm(count):
    return [pl.BlockSpec(memory_space=pltpu.HBM)] * count


def smem(count):
    return [pl.BlockSpec(memory_space=pltpu.SMEM)] * count


def share_kernel(own_ref, down_ref, up_ref, out_ref, wide, turned):
    lane = own_ref[0] * X + own_ref[1]
    wide[...] = down_ref[...].astype(jnp.float32)
    turned[...] = wide[pl.ds(lane // X, 128, stride=2), :].T
    first = pl.multiple_of((lane % X) * SLICE, SLICE)
    down = turned[pl.ds(first, SLICE), :].astype(jnp.bfloat16)
    up = jnp.concatenate([up_ref[...], jnp.zeros((SENT - SLICE - 4, HEAD), jnp.bfloat16)], 0)
    sent = jnp.concatenate([down, up], 0)
    for target in range(GROUPS // 2):
        out_ref[target] = sent


def share(own, down_rows, up_rows):
    return pl.pallas_call(
        share_kernel,
        out_shape=pltpu.HBM((GROUPS // 2, SENT, HEAD), jnp.bfloat16),
        in_specs=smem(1) + vmem(2),
        out_specs=vmem(1)[0],
        scratch_shapes=[
            pltpu.VMEM((2 * 128, RANK), jnp.float32),
            pltpu.VMEM((RANK, 128), jnp.float32),
        ],
        compiler_params=pltpu.CompilerParams(vmem_limit_bytes=VMEM_LIMIT),
        name="share",
    )(own, in_hbm(down_rows), in_hbm(up_rows))


def source_of(own_ref, place):
    x = (own_ref[1] + place * (1 + 2 * own_ref[2])) % X
    return (own_ref[0] + place // X) % 2 * X + x


def places_kernel(lookup_ref, routes_ref, shard_ref, slot_ref):
    for owner in range(GROUPS):
        shard_ref[owner] = lookup_ref[owner]
    target = routes_ref[...]
    later = jnp.broadcast_to(target.astype(jnp.float32), (ROWS, ROWS))
    below = lax.broadcasted_iota(jnp.int32, (ROWS, ROWS), 0)
    after = lax.broadcasted_iota(jnp.int32, (ROWS, ROWS), 1)
    same = jnp.where((later.T == later) & (below < after), 1, 0)
    slot_ref[...] = target * CAP + jnp.sum(same, axis=0, keepdims=True)


def places_of(lookup, routes):
    return pl.pallas_call(
        places_kernel,
        out_shape=(
            pltpu.HBM((GROUPS,), jnp.int32),
            jax.ShapeDtypeStruct((1, ROWS), jnp.int32),
        ),
        in_specs=smem(1) + vmem(1),
        out_specs=(smem(1)[0], vmem(1)[0]),
        cost_estimate=BESIDE,
        compiler_params=pltpu.CompilerParams(vmem_limit_bytes=VMEM_LIMIT),
        name="places",
    )(in_hbm(lookup), in_hbm(routes.reshape(1, ROWS)))


def low_part(own_ref, blocks, down_ref, places):
    total = None
    for block, place in zip(blocks, places):
        first = pl.multiple_of(source_of(own_ref, place) * BLOCK, BLOCK)
        part = lax.dot_general(
            block[...],
            down_ref[:, pl.ds(first, BLOCK)],
            (((1,), (1,)), ((), ())),
            preferred_element_type=jnp.float32,
        )
        total = part if total is None else total + part
    return total


def weight_copies(own_ref, weight_ref, weights, done, places):
    copies = []
    for at, place in enumerate(places):
        first = pl.multiple_of(source_of(own_ref, place) * (2 * BLOCK), 2 * BLOCK)
        copies.append(
            pltpu.make_async_copy(
                weight_ref.at[pl.ds(first, 2 * BLOCK)],
                weights.at[at % BUFFERS],
                done.at[at % BUFFERS],
            )
        )
    return copies


def project_blocks(copies, blocks, weights):
    total = None
    for at, (copy, block) in enumerate(zip(copies, blocks)):
        copy.wait()
        part = jnp.dot(
            block[...],
            weights[at % BUFFERS].reshape(BLOCK, WIDE),
            preferred_element_type=jnp.float32,
        )
        total = part if total is None else total + part
        if at + BUFFERS < len(copies):
            copies[at + BUFFERS].start()
    return total


def low_begin_kernel(
    places, shard_ref, own_ref, near_ref, far_ref, weight_ref, tokens_ref, *refs
):
    down_ref, begun_ref, up_ref, base_ref, up_rows, held, weights, done, weight_done = refs[
        len(places) - 1 :
    ]
    copies = weight_copies(own_ref, weight_ref, weights, weight_done, FIRST)
    for weight_copy in copies[:BUFFERS]:
        weight_copy.start()
    copy = pltpu.make_async_copy(tokens_ref, held, done)
    copy.start()
    core = own_ref[2]
    for chip in range(GROUPS // 2):
        for from_ref, owner in ((near_ref, 2 * chip + core), (far_ref, 2 * chip + 1 - core)):
            shard = shard_ref[owner]
            columns = pl.ds(pl.multiple_of(shard * 128, 128), 128)
            down_ref[:, columns] = from_ref[chip, 0:SLICE, :]
            rows = from_ref[chip, SLICE:SENT, :].astype(jnp.float32)
            up_rows[pl.ds(2 * shard, 2), :] = rows[0:2]
            up_rows[pl.ds(RANK + 2 * shard, 2), :] = rows[2:4]
    up_ref[...] = up_rows[...].astype(jnp.bfloat16)
    copy.wait()
    blocks = [*refs[: len(places) - 1], held]
    begun_ref[...] = low_part(own_ref, blocks, down_ref, places)
    firsts = [blocks[places.index(place)] for place in FIRST]
    base_ref[...] = project_blocks(copies, firsts, weights)


def low_begin(shards, own, near, far, weight_rows, blocks, places):
    return pl.pallas_call(
        functools.partial(low_begin_kernel, places),
        out_shape=(
            jax.ShapeDtypeStruct((SLICE, MODEL), jnp.bfloat16),
            jax.ShapeDtypeStruct((ROWS, SLICE), jnp.float32),
            pltpu.HBM((2 * RANK, HEAD), jnp.bfloat16),
            pltpu.HBM((ROWS, WIDE), jnp.float32),
        ),
        in_specs=smem(2) + vmem(2) + hbm(2) + vmem(len(places) - 1),
        out_specs=tuple(vmem(4)),
        scratch_shapes=[
            pltpu.VMEM((2 * RANK, HEAD), jnp.float32),
            pltpu.VMEM((ROWS, BLOCK), jnp.bfloat16),
            pltpu.VMEM((len(FIRST), 2 * BLOCK, HEAD), jnp.bfloat16),
            pltpu.SemaphoreType.DMA,
            pltpu.SemaphoreType.DMA((len(FIRST),)),
        ],
        compiler_params=pltpu.CompilerParams(vmem_limit_bytes=VMEM_LIMIT),
        name="low_begin",
    )(
        in_hbm(shards),
        own,
        near,
        far,
        weight_rows,
        in_hbm(blocks[0]),
        *[blocks[place] for place in places if place],
    )


def low_end_kernel(places, own_ref, down_ref, begun_ref, *refs):
    total = begun_ref[...] + low_part(own_ref, refs[:-1], down_ref, places)
    low = total.T.astype(jnp.bfloat16)
    for target in range(SHARE):
        refs[-1][target] = low


def low_end(own, down, begun, blocks, places):
    return pl.pallas_call(
        functools.partial(low_end_kernel, places),
        out_shape=pltpu.HBM((SHARE, SLICE, ROWS), jnp.bfloat16),
        in_specs=smem(1) + vmem(2 + len(places)),
        out_specs=vmem(1)[0],
        compiler_params=pltpu.CompilerParams(vmem_limit_bytes=VMEM_LIMIT),
        name="low_end",
    )(own, down, begun, *[blocks[place] for place in places])


def project_kernel(
    places, own_ref, lengths_ref, weight_ref, up_ref, begun_ref, rate_ref, bias_ref, *refs
):
    out_ref, weights, up, begun, weight_done, done = refs[len(places) :]
    copies = weight_copies(own_ref, weight_ref, weights, weight_done, places)
    for copy in copies[:BUFFERS]:
        copy.start()
    small = [
        pltpu.make_async_copy(from_ref, to_ref, done.at[at])
        for at, (from_ref, to_ref) in enumerate(
            [(up_ref, up), (begun_ref, begun)]
        )
    ]
    for copy in small:
        copy.start()
    row = lax.broadcasted_iota(jnp.int32, (ROWS, HEAD), 0)
    begins = jnp.zeros((ROWS, HEAD), jnp.int32)
    start = jnp.int32(0)
    for piece in range(lengths_ref.shape[1]):
        begins = jnp.where(row >= start, jnp.maximum(begins, start), begins)
        start = start + lengths_ref[0, piece]
    angles = (row - begins).astype(jnp.float32) * rate_ref[...]
    low_half = lax.broadcasted_iota(jnp.int32, (ROWS, HEAD), 1) < HEAD // 2
    table = jnp.cos(jnp.where(low_half, angles, angles - np.float32(np.pi / 2)))
    swapped = pltpu.roll(table, HEAD // 2, 1)
    cosine = jnp.where(low_half, table, swapped)
    sine = jnp.where(low_half, -swapped, table)
    out_ref[:, WIDE : WIDE + HEAD] = cosine
    out_ref[:, WIDE + HEAD : 2 * WIDE] = sine
    for copy in small:
        copy.wait()
    out_ref[:, 2 * WIDE :] = up[...].astype(jnp.float32)
    total = begun[...] + project_blocks(copies, refs[: len(places)], weights)
    keys = total[:, :HEAD] + bias_ref[0:1, :].astype(jnp.float32)
    out_ref[:, :HEAD] = keys * cosine + pltpu.roll(keys, HEAD // 2, 1) * sine
    out_ref[:, HEAD:WIDE] = total[:, HEAD:] + bias_ref[1:2, :].astype(jnp.float32)


def project(own, lengths, rate, blocks, places, weight_rows, up, begun, bias):
    return pl.pallas_call(
        functools.partial(project_kernel, places),
        out_shape=jax.ShapeDtypeStruct((ROWS, 2 * WIDE + HEAD), jnp.float32),
        in_specs=smem(2) + hbm(3) + vmem(len(places) + 2),
        out_specs=vmem(1)[0],
        scratch_shapes=[
            pltpu.VMEM((BUFFERS, 2 * BLOCK, HEAD), jnp.bfloat16),
            pltpu.VMEM((2 * RANK, HEAD), jnp.bfloat16),
            pltpu.VMEM((ROWS, WIDE), jnp.float32),
            pltpu.SemaphoreType.DMA((BUFFERS,)),
            pltpu.SemaphoreType.DMA((2,)),
        ],
        compiler_params=pltpu.CompilerParams(vmem_limit_bytes=VMEM_LIMIT),
        name="project",
    )(
        own,
        in_hbm(lengths),
        weight_rows,
        in_hbm(up),
        in_hbm(begun),
        in_hbm(rate),
        in_hbm(bias),
        *[blocks[place] for place in places],
    )


def finish_kernel(made_ref, low_ref, slot_ref, out_ref, placed):
    updates = []
    for side in range(2):
        ranks = slice(side * RANK, (side + 1) * RANK)
        updates.append(
            adapter_scale
            * lax.dot_general(
                low_ref[ranks, :],
                made_ref[ranks, 2 * WIDE :].astype(jnp.bfloat16),
                (((0,), (0,)), ((), ())),
                preferred_element_type=jnp.float32,
            )
        )
    keys = updates[0]
    cosine, sine = made_ref[:, WIDE : WIDE + HEAD], made_ref[:, WIDE + HEAD : 2 * WIDE]
    keys = keys * cosine + pltpu.roll(keys, HEAD // 2, 1) * sine
    rows = made_ref[:, :WIDE] + jnp.concatenate([keys, updates[1]], axis=1)
    rows = rows.astype(jnp.bfloat16)
    slots = lax.broadcasted_iota(jnp.int32, (GROUPS * CAP, ROWS), 0)
    chosen = jnp.where(slots == slot_ref[...], 1.0, 0.0).astype(jnp.bfloat16)
    slot_rows = jnp.dot(chosen, rows, preferred_element_type=jnp.float32)
    for side in range(2):
        placed[pl.ds(side, GROUPS * CAP, stride=2), :] = slot_rows[
            :, side * HEAD : (side + 1) * HEAD
        ]
    out_ref[...] = placed[...].astype(jnp.bfloat16)


def finish(made, low, slots):
    return pl.pallas_call(
        finish_kernel,
        out_shape=jax.ShapeDtypeStruct((2 * GROUPS * CAP, HEAD), jnp.bfloat16),
        in_specs=vmem(3),
        out_specs=vmem(1)[0],
        scratch_shapes=[pltpu.VMEM((2 * GROUPS * CAP, HEAD), jnp.float32)],
        compiler_params=pltpu.CompilerParams(vmem_limit_bytes=VMEM_LIMIT),
        name="finish",
    )(made, low, slots)


def rate_kernel(rate_ref):
    lane = lax.broadcasted_iota(jnp.int32, (1, HEAD), 1) % (HEAD // 2)
    rate_ref[...] = jnp.exp(lane.astype(jnp.float32) * np.float32(-2.0 * np.log(rope_base) / HEAD))


def rates():
    return pl.pallas_call(
        rate_kernel,
        out_shape=pltpu.HBM((1, HEAD), jnp.float32),
        in_specs=[],
        out_specs=vmem(1)[0],
        cost_estimate=BESIDE,
        compiler_params=pltpu.CompilerParams(vmem_limit_bytes=VMEM_LIMIT),
        name="rate",
    )()


def body(tokens, weight, bias, down_blocks, up_blocks, lookup, lengths, routes):
    lane = lax.axis_index("tensor")
    y, x = lane // X, lane % X
    core = lax.axis_index("rollout") % 2
    own = jnp.stack([y, x, core]).astype(jnp.int32)

    weight_rows = in_hbm(weight.reshape(2 * MODEL, HEAD))

    def along_x(block, hop):
        return lax.ppermute(block, ("rollout", "tensor"), X_HOP[hop])

    def across_y(block):
        return lax.ppermute(block, "tensor", Y_PARTNER)

    met = across_y(tokens)
    far_x, next_x, last_x = along_x(tokens, 2), along_x(tokens, 1), along_x(tokens, 3)

    sent = share(own, down_blocks.reshape(2 * 128, RANK), up_blocks.reshape(4, HEAD))
    near = lax.all_to_all(sent, "rollout", 0, 0, tiled=True, axis_index_groups=SAME_CORE)
    far = lax.ppermute(near, "rollout", SIBLING)

    rate = rates()
    far_x, rate = lax.optimization_barrier((far_x, rate))
    shards, slots = places_of(lookup, routes)
    met_far = across_y(far_x)
    met_next, met_last = along_x(met, 1), along_x(met, 3)
    blocks = [tokens, next_x, far_x, last_x, met, met_next, met_far, met_last]
    early, late = (1, 2, 3, 4, 0), (6, 5, 7)
    down, begun, up, started = low_begin(
        shards, own, near, far, weight_rows, blocks, early
    )
    met_far, met_next, met_last, down, begun, up, started, slots = lax.optimization_barrier(
        (met_far, met_next, met_last, down, begun, up, started, slots)
    )
    blocks[5:] = [met_next, met_far, met_last]
    low = low_end(own, down, begun, blocks, late)
    low_all = lax.all_to_all(low, "tensor", 0, 0, tiled=True).reshape(2 * RANK, ROWS)
    made = project(own, lengths, rate, blocks, REST, weight_rows, up, started, bias)
    outgoing = finish(made, low_all, slots)
    arrived = lax.all_to_all(outgoing, "rollout", 0, 0, tiled=True)
    return arrived.reshape(GROUPS * CAP, 2, HEAD)


def solution(mesh):
    in_specs = (
        P("rollout", "tensor"),
        P(None, None, "tensor"),
        P(None, "tensor"),
        P("rollout", None, None),
        P(None, "rollout", "tensor"),
        P(),
        P("rollout", None),
        P("rollout"),
    )
    out_specs = P("rollout", None, "tensor")
    return jax.shard_map(body, mesh=mesh, in_specs=in_specs, out_specs=out_specs, check_vma=False)
```
